32 devices in a mesh: row: 4 (over y, core), col: 8 (over z, x).
Axes of the slice: x: 2, y: 2, z: 4, core: 2. Of those that a mesh axis runs over, the one named last changes fastest.
Arguments:
- rhs: float32 [64, 16384], P(None, ('row', 'col')), may hold values from -6 to 6
- self_term: float32 [16384], P(('row', 'col')), may hold values from 4 to 6
- near_tiles: bfloat16 [4096, 256, 256], P(('row', 'col')), may hold values from -0.0241 to 0.0241
- near_rows: int32 [4096], P(('row', 'col')), may hold values from 0 to 15
- near_cols: int32 [4096], P(('row', 'col')), may hold values from 0 to 7
- near_counts: int32 [32], replicated, may hold values from 1 to 128, as said below
- far_left: bfloat16 [2048, 256, 32], P(('row', 'col')), may hold values from -0.125 to 0.125
- far_right: bfloat16 [2048, 256, 32], P(('row', 'col')), may hold values from -0.125 to 0.125
- far_rows: int32 [2048], P(('row', 'col')), may hold values from 0 to 15
- far_cols: int32 [2048], P(('row', 'col')), may hold values from 0 to 7
- nys_factor: float32 [512, 16384], P(None, ('row', 'col')), may hold values from -0.046875 to 0.046875
- nys_weight: float32 [512], replicated, may hold values from 1 to 16
Outputs:
- solution: float32 [64, 16384], P(None, ('row', 'col'))
- residual: float32 [64, 16384], P(None, ('row', 'col'))
The draws below stay inside these ranges and needn't reach their ends.
Inputs may be any that keep to these rules, and one draw needn't show every extreme that they name: Owner o uses its first near_counts[o] slots; some owner uses all 128.
All inputs are finite; a program needn't handle non-finite values.
Results may differ from the reference program's by a relative error of at most 0.0003.
Values may be sent and summed in bfloat16 or wider, within the bound.
No kernel may reach another device: no remote copies, remote signals or barrier semaphores. Data moves between devices by JAX's collectives and lax.ppermute only.
A program may use at most 128 MiB of HBM per device.

```python
import math
import jax
import jax.numpy as jnp
from jax import lax

BLK = 256
RHS = 64
RANK = 512
PRANK = 32
BLOCKS_DEV = 2
NEAR_MAX = 128
FAR_DEV = 64
ITERS = 2
OWNERS = 32
ORDER = 16384
SLOTS = 4096
FAR_SLOTS = 2048
ROW_BLOCKS = 16
COL_BLOCKS = 8
N_COL = 8


def draw_near_tiles(key, part):
    values = 0.008 * jnp.clip(jax.random.normal(key, (SLOTS, BLK, BLK), jnp.float32), -3.0, 3.0)
    return values.astype(jnp.bfloat16)


def draw_near_counts(key, part):
    first = jax.random.randint(jax.random.fold_in(key, 11), (OWNERS,), 1, NEAR_MAX + 1)
    second = jax.random.randint(jax.random.fold_in(key, 12), (OWNERS,), 1, NEAR_MAX + 1)
    counts = 1 + (first * second - 1) // NEAR_MAX
    busiest = jax.random.randint(jax.random.fold_in(key, 13), (), 0, OWNERS)
    owners = jnp.arange(OWNERS, dtype=jnp.int32)
    return jnp.where(owners == busiest, NEAR_MAX, counts).astype(jnp.int32)


def place_ends(result, key, least, largest):
    longest = result.shape.index(max(result.shape))
    spots = []
    for shift in (0, 1):
        where = [jax.random.randint(jax.random.fold_in(key, axis), (), 0, length) for axis, length in enumerate(result.shape)]
        where[longest] = (where[longest] + shift) % result.shape[longest]
        spots.append(tuple(where))
    return result.at[spots[0]].set(least).at[spots[1]].set(largest)


def steps_of(stream_key, extent, pieces, smallest, top_value):
    gain, own = 1.0, jax.random.fold_in(stream_key, 6)
    for dim, blocks in pieces:
        steps = jnp.exp(jax.random.uniform(jax.random.fold_in(own, dim), (blocks,), jnp.float32, smallest / len(pieces), top_value / len(pieces)))
        gain = gain * jnp.repeat(steps, extent[dim] // blocks).reshape([-1 if axis == dim else 1 for axis in range(len(extent))])
    return gain


def gaussian(stream_key, extent, width, limit, split=(), kind=jnp.bfloat16):
    array = width * jax.random.normal(stream_key, extent, jnp.float32)
    if split:
        array = array * steps_of(stream_key, extent, split, -0.22, 0.18)
    return jnp.clip(array, -limit, limit).astype(kind)


def setup_inputs(seed: int = 0) -> dict:
    key_of = jax.random.split(jax.random.key(seed), 13)
    return {
        "rhs": gaussian(key_of[0], (RHS, ORDER), 1.0, 6.0, ((1, 32),), jnp.float32),
        "self_term": jnp.clip(4.0 + 2.0 * jax.random.uniform(key_of[1], (ORDER,), jnp.float32) ** steps_of(key_of[1], (ORDER,), ((0, 32),), -0.2, 0.2), 4.0, 6.0),
        "near_tiles": draw_near_tiles(jax.random.fold_in(key_of[12], 71), 0),
        "near_rows": place_ends(jax.random.randint(key_of[3], (SLOTS,), 0, ROW_BLOCKS), jax.random.fold_in(key_of[3], 1), 0, ROW_BLOCKS - 1).astype(jnp.int32),
        "near_cols": place_ends(jax.random.randint(key_of[4], (SLOTS,), 0, COL_BLOCKS), jax.random.fold_in(key_of[4], 1), 0, COL_BLOCKS - 1).astype(jnp.int32),
        "near_counts": draw_near_counts(jax.random.fold_in(key_of[12], 71), 0),
        "far_left": gaussian(key_of[6], (FAR_SLOTS, BLK, PRANK), 0.02, 0.125, ((0, 32),)),
        "far_right": gaussian(key_of[7], (FAR_SLOTS, BLK, PRANK), 0.02, 0.125, ((0, 32),)),
        "far_rows": place_ends(jax.random.randint(key_of[8], (FAR_SLOTS,), 0, ROW_BLOCKS), jax.random.fold_in(key_of[8], 1), 0, ROW_BLOCKS - 1).astype(jnp.int32),
        "far_cols": place_ends(jax.random.randint(key_of[9], (FAR_SLOTS,), 0, COL_BLOCKS), jax.random.fold_in(key_of[9], 1), 0, COL_BLOCKS - 1).astype(jnp.int32),
        "nys_factor": gaussian(key_of[10], (RANK, ORDER), ORDER ** -0.5, 0.046875, ((1, 32),), jnp.float32),
        "nys_weight": jnp.clip(jnp.exp(jax.random.uniform(key_of[11], (RANK,), jnp.float32, math.log(1.0), math.log(16.0))), 1.0, 16.0),
    }


def place_blocks(owner, rows, cols):
    grid_row = owner // N_COL
    grid_col = owner % N_COL
    row_glob = grid_row * ROW_BLOCKS + rows
    col_glob = (cols // BLOCKS_DEV * N_COL + grid_col) * BLOCKS_DEV + cols % BLOCKS_DEV
    return (row_glob.astype(jnp.int32), col_glob.astype(jnp.int32))

def operate(direc, self_term, near_tiles, near_rows, near_cols, near_counts, far_left, far_right, far_rows, far_cols):
    nblocks = ORDER // BLK
    blocks = direc.astype(jnp.bfloat16).reshape(RHS, nblocks, BLK).transpose(1, 0, 2).astype(jnp.float32)
    owners = jnp.arange(OWNERS, dtype=jnp.int32)
    slot_ids = jnp.arange(NEAR_MAX, dtype=jnp.int32)

    def near_step(acc, item):
        owner, tiles, rows, cols = item
        row_glob, col_glob = place_blocks(owner, rows, cols)
        mask = (slot_ids < near_counts[owner])[:, None, None]
        tile_f = tiles.astype(jnp.float32)
        forward = jnp.einsum('smk,snk->smn', blocks[col_glob], tile_f)
        transposed = jnp.einsum('smn,snk->smk', blocks[row_glob], tile_f)
        acc = acc.at[row_glob].add(jnp.where(mask, forward, 0.0))
        acc = acc.at[col_glob].add(jnp.where(mask, transposed, 0.0))
        return (acc, None)

    def far_step(acc, item):
        owner, left, right, rows, cols = item
        row_glob, col_glob = place_blocks(owner, rows, cols)
        left_f = left.astype(jnp.float32)
        right_f = right.astype(jnp.float32)
        half_f = jnp.einsum('smk,skr->smr', blocks[col_glob], right_f).astype(jnp.bfloat16)
        half_t = jnp.einsum('smn,snr->smr', blocks[row_glob], left_f).astype(jnp.bfloat16)
        half_f, half_t = lax.optimization_barrier((half_f, half_t))
        forward = jnp.einsum('smr,snr->smn', half_f.astype(jnp.float32), left_f)
        transposed = jnp.einsum('smr,skr->smk', half_t.astype(jnp.float32), right_f)
        acc = acc.at[row_glob].add(forward)
        acc = acc.at[col_glob].add(transposed)
        return (acc, None)
    acc = jnp.zeros((nblocks, RHS, BLK), jnp.float32)
    acc, _ = lax.scan(near_step, acc, (owners, near_tiles.reshape(OWNERS, NEAR_MAX, BLK, BLK), near_rows.reshape(OWNERS, NEAR_MAX), near_cols.reshape(OWNERS, NEAR_MAX)))
    acc, _ = lax.scan(far_step, acc, (owners, far_left.reshape(OWNERS, FAR_DEV, BLK, PRANK), far_right.reshape(OWNERS, FAR_DEV, BLK, PRANK), far_rows.reshape(OWNERS, FAR_DEV), far_cols.reshape(OWNERS, FAR_DEV)))
    return self_term * direc + acc.transpose(1, 0, 2).reshape(RHS, ORDER)

def precondition(resid, nys_factor, nys_weight):
    proj = jnp.dot(resid, nys_factor.T, precision=lax.Precision.HIGHEST)
    return resid + jnp.dot(proj * nys_weight, nys_factor, precision=lax.Precision.HIGHEST)

def chol_solve(matrix, target):
    return jax.scipy.linalg.cho_solve((jnp.linalg.cholesky(matrix), True), target)

def reference(rhs, self_term, near_tiles, near_rows, near_cols, near_counts, far_left, far_right, far_rows, far_cols, nys_factor, nys_weight):
    hp = lax.Precision.HIGHEST
    solution = jnp.zeros_like(rhs)
    residual = rhs
    precond = precondition(residual, nys_factor, nys_weight)
    rho = jnp.dot(residual, precond.T, precision=hp)
    direc = precond
    for step in range(ITERS):
        image = operate(direc, self_term, near_tiles, near_rows, near_cols, near_counts, far_left, far_right, far_rows, far_cols)
        gram = jnp.dot(direc, image.T, precision=hp)
        alpha = chol_solve(gram, rho)
        solution = solution + jnp.dot(alpha.T, direc, precision=hp)
        residual = residual - jnp.dot(alpha.T, image, precision=hp)
        if step + 1 < ITERS:
            precond = precondition(residual, nys_factor, nys_weight)
            rho_next = jnp.dot(residual, precond.T, precision=hp)
            beta = chol_solve(rho, rho_next)
            direc = precond + jnp.dot(beta.T, direc, precision=hp)
            rho = rho_next
    return (solution, residual)
```

```python
import functools

import jax
import jax.numpy as jnp
from jax import lax
from jax.experimental import pallas as pl
from jax.experimental.pallas import tpu as pltpu
from jax.sharding import PartitionSpec as P

F32 = jnp.float32
BF16 = jnp.bfloat16
NN = (((1,), (0,)), ((), ()))
NT = (((1,), (1,)), ((), ()))
TN = (((0,), (0,)), ((), ()))


def exact(left, right, dims):
    return lax.dot_general(
        left, right, dims, precision=lax.Precision.HIGHEST, preferred_element_type=F32
    )


def masks_of(axis):
    return [2**bit for bit in range(lax.axis_size(axis).bit_length() - 1)]


def swap(value, axis, mask):
    pairs = [(source, source ^ mask) for source in range(lax.axis_size(axis))]
    return lax.ppermute(value, axis, pairs)


def place(device, masks):
    spot = jnp.zeros_like(device)
    for mask in masks:
        spot = spot * 2 + (jnp.bitwise_and(device, mask) != 0).astype(jnp.int32)
    return spot


def spread_sum(value):
    axes = ("row", "col")
    devices = lax.axis_size("row") * lax.axis_size("col")
    rows, wanted = value.shape
    step = max(devices * 128 // rows, 128)
    columns = (wanted + step - 1) // step * step
    value = jnp.pad(value, ((0, 0), (0, columns - wanted)))
    tiles = value.reshape(rows // 8, 8, columns // 128, 128).transpose(0, 2, 1, 3)
    pieces = tiles.reshape(devices, -1, 128)
    got = lax.all_to_all(pieces, axes, 0, 0, tiled=True)
    part = jnp.sum(got, axis=0)
    same = jnp.broadcast_to(part[None], pieces.shape)
    full = lax.all_to_all(same, axes, 0, 0, tiled=True)
    tiles = full.reshape(rows // 8, columns // 128, 8, 128).transpose(0, 2, 1, 3)
    return tiles.reshape(rows, columns)[:, :wanted]


def product_kernel(
    forward,
    chunk,
    group,
    count_ref,
    src_ref,
    dst_ref,
    far_src_ref,
    far_dst_ref,
    v_ref,
    inner_ref,
    outer_ref,
    tiles_ref,
    out_ref,
    held,
    arrived,
):
    rhs = v_ref.shape[1]
    depth = held.shape[0]
    count = count_ref[0]
    chunks = lax.div(count + (chunk - 1), chunk)

    def fetch(index):
        slot = lax.rem(index, depth)
        return pltpu.make_async_copy(
            tiles_ref.at[pl.ds(index * chunk, chunk)], held.at[slot], arrived.at[slot]
        )

    for index in range(depth - 1):

        @pl.when(index < chunks)
        def _():
            fetch(index).start()

    out_ref[...] = jnp.zeros_like(out_ref)
    panels = far_src_ref.shape[0]
    prank = inner_ref.shape[0] // panels
    shape = (group * rhs, group * prank)
    of_row = lax.div(lax.broadcasted_iota(jnp.int32, shape, 0), rhs)
    of_lane = lax.div(lax.broadcasted_iota(jnp.int32, shape, 1), prank)
    same = of_row == of_lane

    def far(index, carry):
        start = index * group
        v = jnp.concatenate([v_ref[far_src_ref[start + g]] for g in range(group)], axis=0)
        part = pl.ds(pl.multiple_of(start * prank, group * prank), group * prank)
        half = lax.dot_general(v, inner_ref[part, :], NT, preferred_element_type=F32)
        half = jnp.where(same, half, 0.0).astype(BF16)
        prod = lax.dot_general(half, outer_ref[part, :], NN, preferred_element_type=F32)
        for g in range(group):
            out_ref[far_dst_ref[start + g]] += prod[g * rhs : (g + 1) * rhs]
        return carry

    lax.fori_loop(0, panels // group, far, 0)

    def near(index, carry):
        fetch(index).wait()

        @pl.when(index + (depth - 1) < chunks)
        def _():
            fetch(index + (depth - 1)).start()

        slot = lax.rem(index, depth)
        for s in range(chunk):
            tile = index * chunk + s
            v = v_ref[src_ref[tile]]
            v = jnp.where(tile < count, v, jnp.zeros_like(v))
            out_ref[dst_ref[tile]] += lax.dot_general(
                v, held[slot, s], NT if forward else NN, preferred_element_type=F32
            )
        return carry

    lax.fori_loop(0, chunks, near, 0)


def products(forward, v, tiles, count, src, dst, far_src, far_dst, inner, outer, out_blocks):
    slots, width, _ = tiles.shape
    rhs = v.shape[1]
    chunk, depth, group = 32, 3, 8
    smem = pl.BlockSpec(memory_space=pltpu.SMEM)
    vmem = pl.BlockSpec(memory_space=pltpu.VMEM)
    return pl.pallas_call(
        functools.partial(product_kernel, forward, chunk, group),
        out_shape=jax.ShapeDtypeStruct((out_blocks, rhs, width), F32),
        in_specs=[smem] * 5 + [vmem] * 3 + [pl.BlockSpec(memory_space=pl.ANY)],
        out_specs=vmem,
        scratch_shapes=[
            pltpu.VMEM((depth, chunk, width, width), tiles.dtype),
            pltpu.SemaphoreType.DMA((depth,)),
        ],
        compiler_params=pltpu.CompilerParams(vmem_limit_bytes=40 * 2**20),
        cost_estimate=pl.CostEstimate(
            flops=4 * slots * rhs * width * width,
            bytes_accessed=2 * slots * width * width,
            transcendentals=0,
        ),
        name="forward_products" if forward else "transposed_products",
    )(count.reshape(1), src, dst, far_src, far_dst, v, inner, outer, tiles)


def eliminate(system):
    size = system.shape[0]
    at = lax.broadcasted_iota(jnp.int32, (size, 1), 0)
    for k in range(size):
        pivot_row = system[k : k + 1, :] / system[k : k + 1, k : k + 1]
        system = jnp.where(at == k, pivot_row, system - system[:, k : k + 1] * pivot_row)
    return system[:, size:]


def symmetric(matrix):
    return 0.5 * (matrix + matrix.T)


def project_kernel(rhs_ref, factor_ref, out_ref):
    out_ref[...] = exact(rhs_ref[...], factor_ref[...], NT)


def begin_kernel(rhs_ref, proj_ref, weight_ref, factor_ref, direc_ref, packed_ref):
    direc = rhs_ref[...] + exact(proj_ref[...] * weight_ref[...], factor_ref[...], NN)
    direc_ref[...] = direc
    blocks, _, width = packed_ref.shape
    for b in range(blocks):
        packed_ref[b] = direc[:, b * width : (b + 1) * width].astype(BF16)


def image_of(self_ref, direc_ref, row_ref, col_ref):
    blocks = row_ref.shape[0]
    terms = jnp.concatenate([row_ref[b] + col_ref[b] for b in range(blocks)], axis=1)
    return self_ref[...] * direc_ref[...] + terms


def inner_kernel(
    self_ref, direc_ref, row_ref, col_ref, rhs_ref, factor_ref, image_ref, out_ref
):
    image = image_of(self_ref, direc_ref, row_ref, col_ref)
    image_ref[...] = image
    resid = rhs_ref[...]
    count = resid.shape[0]
    rank = factor_ref.shape[0]
    out_ref[:, :rank] = exact(image, factor_ref[...], NT)
    stack = jnp.concatenate([direc_ref[...], resid, image], axis=0)
    against = exact(stack, image, NT)
    own = exact(resid, resid, NT)
    gram, cross, square = against[:count], against[count : 2 * count], against[2 * count :]
    out_ref[:, rank : rank + 2 * count] = jnp.concatenate([gram, cross], axis=1)
    out_ref[:, rank + 2 * count :] = jnp.concatenate([square, own], axis=1)


def advance_kernel(
    sums_ref,
    proj_ref,
    weight_ref,
    factor_ref,
    rhs_ref,
    direc_ref,
    image_ref,
    solution_ref,
    resid_ref,
    next_ref,
    packed_ref,
    rho_ref,
):
    count = rhs_ref.shape[0]
    rank = factor_ref.shape[0]
    image_proj = sums_ref[:, :rank]
    pair = sums_ref[:, rank : rank + 2 * count]
    gram, cross = pair[:, :count], pair[:, count:]
    pair = sums_ref[:, rank + 2 * count :]
    square, own = pair[:, :count], pair[:, count:]
    weight = weight_ref[...]
    proj = proj_ref[...]
    rho = own + exact(proj * weight, proj, NT)
    unit = (
        lax.broadcasted_iota(jnp.int32, (count, count), 0)
        == lax.broadcasted_iota(jnp.int32, (count, count), 1)
    ).astype(F32)
    alpha = eliminate(jnp.concatenate([symmetric(gram), rho], axis=1))
    inverse = eliminate(jnp.concatenate([symmetric(rho), unit], axis=1))
    alpha_t = alpha.T
    proj = proj - exact(alpha_t, image_proj, NN)
    mixed = exact(cross, alpha, NN)
    new = own - mixed - mixed.T + exact(exact(alpha_t, square, NN), alpha, NN)
    new = new + exact(proj * weight, proj, NT)
    beta = exact(inverse, new, NN)
    direc = direc_ref[...]
    resid = rhs_ref[...] - exact(alpha_t, image_ref[...], NN)
    after = resid + exact(proj * weight, factor_ref[...], NN) + exact(beta.T, direc, NN)
    solution_ref[...] = exact(alpha_t, direc, NN)
    resid_ref[...] = resid
    next_ref[...] = after
    rho_ref[...] = new
    blocks, _, width = packed_ref.shape
    for b in range(blocks):
        packed_ref[b] = after[:, b * width : (b + 1) * width].astype(BF16)


def last_image_kernel(self_ref, direc_ref, row_ref, col_ref, image_ref, gram_ref):
    image = image_of(self_ref, direc_ref, row_ref, col_ref)
    image_ref[...] = image
    gram = exact(direc_ref[...], image, NT)
    gram_ref[...] = jnp.concatenate([gram, jnp.zeros_like(gram)], axis=1)


def finish_kernel(
    gram_ref, rho_ref, solution_ref, resid_ref, direc_ref, image_ref, out_ref, left_ref
):
    count = rho_ref.shape[0]
    gram = gram_ref[:, :count]
    alpha = eliminate(jnp.concatenate([symmetric(gram), rho_ref[...]], axis=1))
    alpha_t = alpha.T
    out_ref[...] = solution_ref[...] + exact(alpha_t, direc_ref[...], NN)
    left_ref[...] = resid_ref[...] - exact(alpha_t, image_ref[...], NN)


def call(kernel, outs, name, *operands):
    return pl.pallas_call(
        kernel,
        out_shape=[jax.ShapeDtypeStruct(shape, dtype) for shape, dtype in outs],
        compiler_params=pltpu.CompilerParams(vmem_limit_bytes=40 * 2**20),
        name=name,
    )(*operands)


def local(
    rhs,
    self_term,
    near_tiles,
    near_rows,
    near_cols,
    near_counts,
    far_left,
    far_right,
    far_rows,
    far_cols,
    nys_factor,
    nys_weight,
):
    width = near_tiles.shape[1]
    count_rhs, columns = rhs.shape
    blocks = columns // width
    n_row, n_col = lax.axis_size("row"), lax.axis_size("col")
    grid_row, grid_col = lax.axis_index("row"), lax.axis_index("col")
    count = near_counts[grid_row * n_col + grid_col]
    rank = nys_factor.shape[0]
    self_row = self_term.reshape(1, columns)
    weight = nys_weight.reshape(1, rank)
    prank = far_left.shape[2]
    left = far_left.transpose(0, 2, 1).reshape(-1, width)
    right = far_right.transpose(0, 2, 1).reshape(-1, width)

    col_masks, row_masks = masks_of("col"), masks_of("row")
    gather_col, gather_row = col_masks[::-1], row_masks[::-1]
    path_a = col_masks[-2::-1] + col_masks[-1:]
    path_b = col_masks
    scatter_row = row_masks

    def relative(ids, me):
        return jnp.bitwise_xor(ids // blocks, me), ids % blocks

    def gathered(ids, me, masks):
        device, block = relative(ids, me)
        return place(device, masks[::-1]) * blocks + block

    def scattered_col(ids):
        device, block = relative(ids, grid_col)
        path = jnp.where(block % 2 == 0, place(device, path_a), place(device, path_b))
        return block * n_col + path

    def scattered_row(ids):
        device, block = relative(ids, grid_row)
        return place(device, scatter_row) * blocks + block

    row_src = gathered(near_rows, grid_col, gather_col)
    col_src = gathered(near_cols, grid_row, gather_row)
    far_row_src = gathered(far_rows, grid_col, gather_col)
    far_col_src = gathered(far_cols, grid_row, gather_row)
    row_dst, far_row_dst = scattered_col(near_rows), scattered_col(far_rows)
    col_dst, far_col_dst = scattered_row(near_cols), scattered_row(far_cols)

    def operate(packed):
        col_side = row_side = packed
        for axis_step in range(max(len(gather_col), len(gather_row))):
            if axis_step < len(gather_row):
                got = swap(col_side, "row", gather_row[axis_step])
                col_side = jnp.concatenate([col_side, got], axis=0)
            if axis_step < len(gather_col):
                got = swap(row_side, "col", gather_col[axis_step])
                row_side = jnp.concatenate([row_side, got], axis=0)
        forward = products(
            True, col_side, near_tiles, count, col_src, row_dst,
            far_col_src, far_row_dst, right, left, n_col * blocks,
        )
        transposed = products(
            False, row_side, near_tiles, count, row_src, col_dst,
            far_row_src, far_col_dst, left, right, n_row * blocks,
        )
        parts = [forward[b * n_col : (b + 1) * n_col] for b in range(blocks)]
        for step in range(len(col_masks)):
            for b in range(blocks):
                mask = (path_a if b % 2 == 0 else path_b)[step]
                half = parts[b].shape[0] // 2
                parts[b] = parts[b][:half] + swap(parts[b][half:], "col", mask)
        for mask in scatter_row:
            half = transposed.shape[0] // 2
            transposed = transposed[:half] + swap(transposed[half:], "row", mask)
        return jnp.concatenate(parts, axis=0), transposed

    full, pack = (count_rhs, columns), (blocks, count_rhs, width)
    square = (count_rhs, count_rhs)
    (partial,) = call(
        project_kernel, [((count_rhs, rank), F32)], "project", rhs, nys_factor
    )
    proj = spread_sum(partial)
    direc, packed = call(
        begin_kernel, [(full, F32), (pack, BF16)], "begin", rhs, proj, weight, nys_factor
    )
    row_part, col_part = operate(packed)
    image, partial = call(
        inner_kernel, [(full, F32), ((count_rhs, rank + 4 * count_rhs), F32)], "inner",
        self_row, direc, row_part, col_part, rhs, nys_factor,
    )
    sums = spread_sum(partial)
    solution, residual, direc, packed, rho = call(
        advance_kernel, [(full, F32), (full, F32), (full, F32), (pack, BF16), (square, F32)],
        "advance", sums, proj, weight, nys_factor, rhs, direc, image,
    )
    row_part, col_part = operate(packed)
    image, partial = call(
        last_image_kernel, [(full, F32), ((count_rhs, 2 * count_rhs), F32)], "last_image",
        self_row, direc, row_part, col_part,
    )
    gram = spread_sum(partial)
    return tuple(
        call(
            finish_kernel, [(full, F32), (full, F32)], "finish",
            gram, rho, solution, residual, direc, image,
        )
    )


def solution(mesh):
    in_specs = (
        P(None, ("row", "col")),
        P(("row", "col")),
        P(("row", "col"), None, None),
        P(("row", "col")),
        P(("row", "col")),
        P(),
        P(("row", "col"), None, None),
        P(("row", "col"), None, None),
        P(("row", "col")),
        P(("row", "col")),
        P(None, ("row", "col")),
        P(),
    )
    out_specs = (P(None, ("row", "col")), P(None, ("row", "col")))
    return jax.shard_map(local, mesh=mesh, in_specs=in_specs, out_specs=out_specs, check_vma=False)
```

```python
import functools

import jax
import jax.numpy as jnp
from jax import lax
from jax.experimental import pallas as pl
from jax.experimental.pallas import tpu as pltpu
from jax.sharding import PartitionSpec as P

F32 = jnp.float32
BF16 = jnp.bfloat16
NN = (((1,), (0,)), ((), ()))
NT = (((1,), (1,)), ((), ()))
VMEM_LIMIT = 44 * 2**20


def exact(left, right, dims):
    return lax.dot_general(
        left, right, dims, precision=lax.Precision.HIGHEST, preferred_element_type=F32
    )


def masks_of(axis):
    return [2**bit for bit in range(lax.axis_size(axis).bit_length() - 1)]


def swap(value, axis, mask):
    pairs = [(source, source ^ mask) for source in range(lax.axis_size(axis))]
    return lax.ppermute(value, axis, pairs)


def place(device, masks):
    spot = jnp.zeros_like(device)
    for mask in masks:
        spot = spot * 2 + (jnp.bitwise_and(device, mask) != 0).astype(jnp.int32)
    return spot


def pieces_shape(rows, columns, devices):
    return (devices, 2 * rows // devices, columns // 2)


def to_pieces(value, pieces_ref):
    pieces, depth, width = pieces_ref.shape
    for piece in range(pieces):
        row, half = piece // 2 * depth, piece % 2 * width
        pieces_ref[piece] = value[row : row + depth, half : half + width]


def from_pieces(pieces_ref):
    pieces = pieces_ref.shape[0]
    halves = [[pieces_ref[p] for p in range(side, pieces, 2)] for side in (0, 1)]
    return jnp.concatenate([jnp.concatenate(half, axis=0) for half in halves], axis=1)


def total_kernel(got_ref, out_ref):
    total = got_ref[0]
    for piece in range(1, got_ref.shape[0]):
        total = total + got_ref[piece]
    for piece in range(got_ref.shape[0]):
        out_ref[piece] = total


def spread_sum(pieces):
    axes = ("row", "col")
    got = lax.all_to_all(pieces, axes, 0, 0, tiled=True)
    (same,) = call(total_kernel, [(pieces.shape, F32)], "total", [], [got])
    return lax.all_to_all(same, axes, 0, 0, tiled=True)


def product_kernel(
    forward,
    chunk,
    group,
    count_ref,
    src_ref,
    dst_ref,
    far_src_ref,
    far_dst_ref,
    v_ref,
    inner_hbm,
    outer_hbm,
    tiles_ref,
    out_ref,
    inner_ref,
    outer_ref,
    held,
    far_arrived,
    arrived,
):
    rhs = v_ref.shape[1]
    depth = held.shape[0]
    count = count_ref[0]
    chunks = lax.div(count + (chunk - 1), chunk)

    def fetch(index):
        slot = lax.rem(index, depth)
        return pltpu.make_async_copy(
            tiles_ref.at[pl.ds(index * chunk, chunk)], held.at[slot], arrived.at[slot]
        )

    far_copies = [
        pltpu.make_async_copy(inner_hbm, inner_ref, far_arrived.at[0]),
        pltpu.make_async_copy(outer_hbm, outer_ref, far_arrived.at[1]),
    ]
    for copy in far_copies:
        copy.start()
    for index in range(depth - 1):

        @pl.when(index < chunks)
        def _():
            fetch(index).start()

    out_ref[...] = jnp.zeros_like(out_ref)
    panels = far_src_ref.shape[0]
    prank = inner_ref.shape[0] // panels
    shape = (group * rhs, group * prank)
    of_row = lax.div(lax.broadcasted_iota(jnp.int32, shape, 0), rhs)
    of_lane = lax.div(lax.broadcasted_iota(jnp.int32, shape, 1), prank)
    same = of_row == of_lane

    for copy in far_copies:
        copy.wait()
    for start in range(0, panels, group):
        v = jnp.concatenate([v_ref[far_src_ref[start + g]] for g in range(group)], axis=0)
        part = pl.ds(start * prank, group * prank)
        half = lax.dot_general(v, inner_ref[part, :], NT, preferred_element_type=F32)
        half = jnp.where(same, half, 0.0).astype(BF16)
        prod = lax.dot_general(half, outer_ref[part, :], NN, preferred_element_type=F32)
        for g in range(group):
            out_ref[far_dst_ref[start + g]] += prod[g * rhs : (g + 1) * rhs]

    def near(index, carry):
        fetch(index).wait()

        @pl.when(index + (depth - 1) < chunks)
        def _():
            fetch(index + (depth - 1)).start()

        slot = lax.rem(index, depth)
        for s in range(chunk):
            tile = index * chunk + s
            v = v_ref[src_ref[tile]]
            v = jnp.where(tile < count, v, jnp.zeros_like(v))
            out_ref[dst_ref[tile]] += lax.dot_general(
                v, held[slot, s], NT if forward else NN, preferred_element_type=F32
            )
        return carry

    lax.fori_loop(0, chunks, near, 0)


def products(forward, v, tiles, count, src, dst, far_src, far_dst, inner, outer, out_blocks):
    slots, width, _ = tiles.shape
    rhs = v.shape[1]
    chunk, depth, group = 32, 3, 8
    smem = pl.BlockSpec(memory_space=pltpu.SMEM)
    vmem = pl.BlockSpec(memory_space=pltpu.VMEM)
    return pl.pallas_call(
        functools.partial(product_kernel, forward, chunk, group),
        out_shape=jax.ShapeDtypeStruct((out_blocks, rhs, width), F32),
        in_specs=[smem] * 5 + [vmem] + [pl.BlockSpec(memory_space=pltpu.HBM)] * 3,
        out_specs=vmem,
        scratch_shapes=[
            pltpu.VMEM(inner.shape, inner.dtype),
            pltpu.VMEM(outer.shape, outer.dtype),
            pltpu.VMEM((depth, chunk, width, width), tiles.dtype),
            pltpu.SemaphoreType.DMA((2,)),
            pltpu.SemaphoreType.DMA((depth,)),
        ],
        compiler_params=pltpu.CompilerParams(vmem_limit_bytes=VMEM_LIMIT),
        cost_estimate=pl.CostEstimate(
            flops=4 * slots * rhs * width * width,
            bytes_accessed=2 * slots * width * width,
            transcendentals=0,
        ),
        name="forward_products" if forward else "transposed_products",
    )(count.reshape(1), src, dst, far_src, far_dst, v, inner, outer, tiles)


def eliminate(systems, block=4):
    size, lanes = systems[0].shape
    parts = [[s[t : t + 8, :] for t in range(0, size, 8)] for s in systems]
    sub = lax.broadcasted_iota(jnp.int32, (8, lanes), 0)
    every = range(block)
    for k in range(0, size, block):
        home, offset = k // 8, k % 8
        for n, part in enumerate(parts):
            cols = [[jnp.broadcast_to(p[:, k + j : k + j + 1], p.shape) for p in part] for j in every]
            head = part[home]
            rows = [jnp.broadcast_to(head[offset + i : offset + i + 1, :], head.shape) for i in every]
            small = [
                [jnp.broadcast_to(cols[j][home][offset + i : offset + i + 1, :], head.shape) for j in every]
                for i in every
            ]
            for p in every:
                inverse = 1.0 / small[p][p]
                rows[p] = rows[p] * inverse
                for j in range(p + 1, block):
                    small[p][j] = small[p][j] * inverse
                for i in every:
                    if i != p:
                        factor = small[i][p]
                        rows[i] = rows[i] - factor * rows[p]
                        for j in range(p + 1, block):
                            small[i][j] = small[i][j] - factor * small[p][j]
            for t in range(len(part)):
                value = part[t]
                for j in every:
                    value = value - cols[j][t] * rows[j]
                part[t] = value
            for i in every:
                part[home] = jnp.where(sub == offset + i, rows[i], part[home])
    return [jnp.concatenate(part, axis=0)[:, size:] for part in parts]


def symmetric(matrix):
    return 0.5 * (matrix + matrix.T)


def call(kernel, outs, name, far, near, after=()):
    def body(*refs):
        refs = refs[len(after) :]
        sources, refs = refs[: len(far)], refs[len(far) :]
        given, refs = refs[: len(near)], refs[len(near) :]
        results, refs = refs[: len(outs)], refs[len(outs) :]
        held = refs[: len(far)]
        copies = [
            pltpu.make_async_copy(source, target, refs[-1].at[index])
            for index, (source, target) in enumerate(zip(sources, held))
        ]
        for copy in copies:
            copy.start()

        def reader(index):
            def read():
                copies[index].wait()
                return held[index][...]

            return read

        kernel(*[reader(index) for index in range(len(far))], *given, *results)

    vmem = pl.BlockSpec(memory_space=pltpu.VMEM)
    return pl.pallas_call(
        body,
        out_shape=[jax.ShapeDtypeStruct(shape, dtype) for shape, dtype in outs],
        in_specs=[pl.BlockSpec(memory_space=pl.ANY)] * len(after)
        + [pl.BlockSpec(memory_space=pltpu.HBM)] * len(far)
        + [vmem] * len(near),
        out_specs=[vmem] * len(outs),
        scratch_shapes=[pltpu.VMEM(value.shape, value.dtype) for value in far]
        + [pltpu.SemaphoreType.DMA((max(len(far), 1),))],
        compiler_params=pltpu.CompilerParams(vmem_limit_bytes=VMEM_LIMIT),
        name=name,
    )(*after, *far, *near)


def pack(direc, packed_ref):
    blocks, _, width = packed_ref.shape
    for b in range(blocks):
        packed_ref[b] = direc[:, b * width : (b + 1) * width].astype(BF16)


def project_kernel(rhs, factor, out_ref):
    to_pieces(exact(rhs(), factor(), NT), out_ref)


def begin_kernel(rhs, weight, factor, proj_ref, direc_ref, packed_ref):
    proj = from_pieces(proj_ref)
    direc = rhs() + exact(proj * weight(), factor(), NN)
    direc_ref[...] = direc
    pack(direc, packed_ref)


def image_of(self_term, direc, terms):
    sums = [own[...] + got[...] for own, got in terms]
    row_terms, col_terms = jnp.concatenate(sums[:-1], axis=0), sums[-1]
    both = row_terms + col_terms
    return self_term * direc + jnp.concatenate([both[b] for b in range(both.shape[0])], axis=1)


def paired(refs):
    return list(zip(refs[::2], refs[1::2]))


def fold_kernel(forward_ref, *refs):
    blocks = len(refs) // 3
    half, width = refs[0].shape[0], refs[0].shape[0] // 2
    for b in range(blocks):
        start = 2 * half * b
        for part in range(2):
            mine = forward_ref[start + part * width : start + (part + 1) * width]
            got = refs[b][part * width : (part + 1) * width]
            refs[blocks + 2 * b + part][...] = mine + got


def inner_kernel(self_term, rhs, factor, direc_ref, *refs):
    terms, (image_ref, out_ref) = paired(refs[:-2]), refs[-2:]
    direc = direc_ref[...]
    image = image_of(self_term(), direc, terms)
    image_ref[...] = image
    resid = rhs()
    count = resid.shape[0]
    stack = jnp.concatenate([direc, resid, image], axis=0)
    against = exact(stack, image, NT)
    own = exact(resid, resid, NT)
    pairs = jnp.concatenate(
        [against[:count], against[count : 2 * count], against[2 * count :], own], axis=1
    )
    to_pieces(jnp.concatenate([exact(image, factor(), NT), pairs], axis=1), out_ref)


def advance_kernel(
    weight_of,
    factor,
    rhs,
    sums_ref,
    proj_ref,
    direc_ref,
    image_ref,
    solution_ref,
    resid_ref,
    next_ref,
    packed_ref,
    rho_ref,
):
    count = rho_ref.shape[0]
    weight, proj, sums = weight_of(), from_pieces(proj_ref), from_pieces(sums_ref)
    rank = proj.shape[1]
    image_proj = sums[:, :rank]
    gram, cross, square, own = (
        sums[:, rank + count * index : rank + count * (index + 1)] for index in range(4)
    )
    rho = own + exact(proj * weight, proj, NT)
    unit = (
        lax.broadcasted_iota(jnp.int32, (count, count), 0)
        == lax.broadcasted_iota(jnp.int32, (count, count), 1)
    ).astype(F32)
    alpha, inverse = eliminate(
        [
            jnp.concatenate([symmetric(gram), rho], axis=1),
            jnp.concatenate([symmetric(rho), unit], axis=1),
        ]
    )
    alpha_t = alpha.T
    proj = proj - exact(alpha_t, image_proj, NN)
    mixed = exact(cross, alpha, NN)
    new = own - mixed - mixed.T + exact(exact(alpha_t, square, NN), alpha, NN)
    new = new + exact(proj * weight, proj, NT)
    beta = exact(inverse, new, NN)
    direc = direc_ref[...]
    resid = rhs() - exact(alpha_t, image_ref[...], NN)
    after = resid + exact(proj * weight, factor(), NN) + exact(beta.T, direc, NN)
    pack(after, packed_ref)
    solution_ref[...] = exact(alpha_t, direc, NN)
    resid_ref[...] = resid
    next_ref[...] = after
    rho_ref[...] = new


def last_image_kernel(self_term, direc_ref, *refs):
    terms, (image_ref, gram_ref) = paired(refs[:-2]), refs[-2:]
    direc = direc_ref[...]
    image = image_of(self_term(), direc, terms)
    image_ref[...] = image
    gram = exact(direc, image, NT)
    to_pieces(jnp.concatenate([gram] + [jnp.zeros_like(gram)] * 3, axis=1), gram_ref)


def finish_kernel(
    gram_ref, rho_ref, solution_ref, resid_ref, direc_ref, image_ref, out_ref, left_ref
):
    count = rho_ref.shape[0]
    gram = from_pieces(gram_ref)[:, :count]
    (alpha,) = eliminate([jnp.concatenate([symmetric(gram), rho_ref[...]], axis=1)])
    alpha_t = alpha.T
    out_ref[...] = solution_ref[...] + exact(alpha_t, direc_ref[...], NN)
    left_ref[...] = resid_ref[...] - exact(alpha_t, image_ref[...], NN)


def local(
    rhs,
    self_term,
    near_tiles,
    near_rows,
    near_cols,
    near_counts,
    far_left,
    far_right,
    far_rows,
    far_cols,
    nys_factor,
    nys_weight,
):
    width = near_tiles.shape[1]
    count_rhs, columns = rhs.shape
    blocks = columns // width
    n_row, n_col = lax.axis_size("row"), lax.axis_size("col")
    grid_row, grid_col = lax.axis_index("row"), lax.axis_index("col")
    count = near_counts[grid_row * n_col + grid_col]
    rank = nys_factor.shape[0]
    self_row = self_term.reshape(1, columns)
    weight = nys_weight.reshape(1, rank)
    prank = far_left.shape[2]
    left = far_left.transpose(0, 2, 1).reshape(-1, width)
    right = far_right.transpose(0, 2, 1).reshape(-1, width)

    col_masks, row_masks = masks_of("col"), masks_of("row")
    gather_col, gather_row = col_masks[::-1], row_masks[::-1]
    path_a = col_masks[-2::-1] + col_masks[-1:]
    path_b = col_masks
    scatter_row = row_masks

    def relative(ids, me):
        return jnp.bitwise_xor(ids // blocks, me), ids % blocks

    def gathered(ids, me, masks):
        device, block = relative(ids, me)
        return place(device, masks[::-1]) * blocks + block

    def scattered_col(ids):
        device, block = relative(ids, grid_col)
        path = jnp.where(block % 2 == 0, place(device, path_a), place(device, path_b))
        return block * n_col + path

    def scattered_row(ids):
        device, block = relative(ids, grid_row)
        return place(device, scatter_row) * blocks + block

    row_src = gathered(near_rows, grid_col, gather_col)
    col_src = gathered(near_cols, grid_row, gather_row)
    far_row_src = gathered(far_rows, grid_col, gather_col)
    far_col_src = gathered(far_cols, grid_row, gather_row)
    row_dst, far_row_dst = scattered_col(near_rows), scattered_col(far_rows)
    col_dst, far_col_dst = scattered_row(near_cols), scattered_row(far_cols)

    def operate(packed):
        col_side = row_side = packed
        for axis_step in range(max(len(gather_col), len(gather_row))):
            if axis_step < len(gather_row):
                got = swap(col_side, "row", gather_row[axis_step])
                col_side = jnp.concatenate([col_side, got], axis=0)
            if axis_step < len(gather_col):
                got = swap(row_side, "col", gather_col[axis_step])
                row_side = jnp.concatenate([row_side, got], axis=0)
        forward = products(
            True, col_side, near_tiles, count, col_src, row_dst,
            far_col_src, far_row_dst, right, left, n_col * blocks,
        )
        transposed = products(
            False, row_side, near_tiles, count, row_src, col_dst,
            far_row_src, far_col_dst, left, right, n_row * blocks,
        )

        def halve(value, axis, mask):
            half = value.shape[0] // 2
            return value[:half], swap(value[half:], axis, mask)

        half = n_col // 2
        sends = [forward[b * n_col + half : (b + 1) * n_col] for b in range(blocks)]
        paths = [path_a if b % 2 == 0 else path_b for b in range(blocks)]
        got = [swap(sends[b], "col", paths[b][0]) for b in range(blocks)]
        quarter = (half // 2, count_rhs, width)
        folded = call(
            fold_kernel, [(quarter, F32)] * (2 * blocks), "fold", [], [forward, *got], [transposed]
        )
        pairs = [
            (folded[2 * b], swap(folded[2 * b + 1], "col", paths[b][1])) for b in range(blocks)
        ]
        for step in range(2, len(col_masks)):
            parts = [own + other for own, other in pairs]
            pairs = [halve(parts[b], "col", paths[b][step]) for b in range(blocks)]
        for mask in scatter_row:
            last = halve(transposed, "row", mask)
            transposed = last[0] + last[1]
        return [term for pair in pairs + [last] for term in pair]

    devices = n_row * n_col
    full, packs = (count_rhs, columns), (blocks, count_rhs, width)
    shape_of = lambda wanted: pieces_shape(count_rhs, wanted, devices)
    (partial,) = call(
        project_kernel, [(shape_of(rank), F32)], "project", [rhs, nys_factor], []
    )
    proj = spread_sum(partial)
    direc, packed = call(
        begin_kernel, [(full, F32), (packs, BF16)], "begin", [rhs, weight, nys_factor], [proj]
    )
    terms = operate(packed)
    image, partial = call(
        inner_kernel, [(full, F32), (shape_of(rank + 4 * count_rhs), F32)], "inner",
        [self_row, rhs, nys_factor], [direc, *terms],
    )
    sums = spread_sum(partial)
    solution, residual, direc, packed, rho = call(
        advance_kernel,
        [(full, F32), (full, F32), (full, F32), (packs, BF16), ((count_rhs, count_rhs), F32)],
        "advance", [weight, nys_factor, rhs], [sums, proj, direc, image],
    )
    terms = operate(packed)
    image, partial = call(
        last_image_kernel, [(full, F32), (shape_of(4 * count_rhs), F32)], "last_image",
        [self_row], [direc, *terms],
    )
    gram = spread_sum(partial)
    return tuple(
        call(
            finish_kernel, [(full, F32), (full, F32)], "finish",
            [], [gram, rho, solution, residual, direc, image],
        )
    )


def solution(mesh):
    in_specs = (
        P(None, ("row", "col")),
        P(("row", "col")),
        P(("row", "col"), None, None),
        P(("row", "col")),
        P(("row", "col")),
        P(),
        P(("row", "col"), None, None),
        P(("row", "col"), None, None),
        P(("row", "col")),
        P(("row", "col")),
        P(None, ("row", "col")),
        P(),
    )
    out_specs = (P(None, ("row", "col")), P(None, ("row", "col")))
    return jax.shard_map(local, mesh=mesh, in_specs=in_specs, out_specs=out_specs, check_vma=False)
```

```python
import functools

import jax
import jax.numpy as jnp
from jax import lax
from jax.experimental import pallas as pl
from jax.experimental.pallas import tpu as pltpu
from jax.sharding import PartitionSpec as P

F32 = jnp.float32
BF16 = jnp.bfloat16
NN = (((1,), (0,)), ((), ()))
NT = (((1,), (1,)), ((), ()))
VMEM_LIMIT = 18 * 2**20
PROJECT_LIMIT = 62 * 2**20
STREAM_LIMIT = 36 * 2**20
GROUP = 8


def exact(left, right, dims):
    return lax.dot_general(
        left, right, dims, precision=lax.Precision.HIGHEST, preferred_element_type=F32
    )


def masks_of(axis):
    return [2**bit for bit in range(lax.axis_size(axis).bit_length() - 1)]


def swap(value, axis, mask):
    pairs = [(source, source ^ mask) for source in range(lax.axis_size(axis))]
    return lax.ppermute(value, axis, pairs)


def place(device, masks):
    spot = jnp.zeros_like(device)
    for mask in masks:
        spot = spot * 2 + (jnp.bitwise_and(device, mask) != 0).astype(jnp.int32)
    return spot


def pieces_shape(rows, columns, devices):
    return (devices, 2 * rows // devices, columns // 2)


def to_pieces(value, pieces_ref):
    pieces, depth, width = pieces_ref.shape
    for piece in range(pieces):
        row, half = piece // 2 * depth, piece % 2 * width
        pieces_ref[piece] = value[row : row + depth, half : half + width]


def from_pieces(pieces_ref):
    pieces = pieces_ref.shape[0]
    halves = [[pieces_ref[p] for p in range(side, pieces, 2)] for side in (0, 1)]
    return jnp.concatenate([jnp.concatenate(half, axis=0) for half in halves], axis=1)


def total_kernel(got_ref, out_ref):
    total = got_ref[0]
    for piece in range(1, got_ref.shape[0]):
        total = total + got_ref[piece]
    for piece in range(got_ref.shape[0]):
        out_ref[piece] = total


def spread_sum(pieces):
    axes = ("row", "col")
    got = lax.all_to_all(pieces, axes, 0, 0, tiled=True)
    (same,) = call(total_kernel, [(pieces.shape, F32)], "total", [got])
    return lax.all_to_all(same, axes, 0, 0, tiled=True)


def near_kernel(forward, chunk, stream, part, count_ref, src_ref, dst_ref, v_ref, tiles_ref, *refs):
    count = count_ref[0]
    chunks = lax.div(count + (chunk - 1), chunk)
    slots = tiles_ref.shape[0]
    if stream:
        out_ref, held_ref, arrived = refs

        def fetch(index):
            part = pl.ds(index * chunk, chunk)
            return pltpu.make_async_copy(
                tiles_ref.at[part], held_ref.at[part], arrived.at[index]
            )

        for index in range(slots // chunk):

            @pl.when(index < chunks)
            def _():
                fetch(index).start()

    else:
        out_ref, held_ref = refs[-1], tiles_ref
    out_ref[...] = jnp.zeros_like(out_ref) if stream or len(refs) == 1 else refs[0][...]

    first, last = (lax.min(chunks, slots // chunk * (part[0] + end) // part[1]) for end in (0, 1))

    def near(index, carry):
        if stream:
            fetch(index).wait()
        for s in range(chunk):
            tile = index * chunk + s
            v = v_ref[src_ref[tile]]
            v = jnp.where(tile < count, v, jnp.zeros_like(v))
            out_ref[dst_ref[tile]] += lax.dot_general(
                v, held_ref[tile], NT if forward else NN, preferred_element_type=F32
            )
        return carry

    lax.fori_loop(first, last, near, 0)
    if stream:

        def rest(index, carry):
            fetch(index).wait()
            return carry

        lax.fori_loop(last, chunks, rest, 0)


def near_products(
    forward, v, tiles, count, src, dst, part=(0, 1), out_blocks=None, start=None, stream=False, after=(),
    far=(),
):
    slots, width, _ = tiles.shape
    rhs = v.shape[1]
    chunk = 32

    def body(*refs):
        far_refs, refs = refs[len(after) : len(after) + len(far)], refs[len(after) + len(far) :]
        near_kernel(forward, chunk, stream, part, *refs)
        if far:
            src, dst, inner, outer = far_refs
            add_far(GROUP, src, dst, refs[3], inner, outer, refs[-1])

    extra = [] if start is None else [start]
    total = jax.ShapeDtypeStruct((out_blocks, rhs, width) if start is None else start.shape, F32)
    smem = pl.BlockSpec(memory_space=pltpu.SMEM)
    vmem = pl.BlockSpec(memory_space=pltpu.VMEM)
    hbm = pl.BlockSpec(memory_space=pltpu.HBM)
    return pl.pallas_call(
        body,
        out_shape=[total, jax.ShapeDtypeStruct(tiles.shape, tiles.dtype)] if stream else [total],
        in_specs=[pl.BlockSpec(memory_space=pl.ANY)] * len(after)
        + ([smem] * 2 + [vmem] * 2 if far else [])
        + [smem] * 3
        + [vmem]
        + [hbm if stream else vmem]
        + [vmem] * len(extra),
        out_specs=[vmem, vmem] if stream else [vmem],
        scratch_shapes=[pltpu.SemaphoreType.DMA((slots // chunk,))] if stream else [],
        compiler_params=pltpu.CompilerParams(vmem_limit_bytes=STREAM_LIMIT if stream else VMEM_LIMIT),
        cost_estimate=pl.CostEstimate(
            flops=4 * slots * rhs * width * width,
            bytes_accessed=2 * slots * width * width,
            transcendentals=0,
        ),
        name="near_forward" if forward else "near_transposed",
    )(*after, *far, count, src, dst, v, tiles, *extra)


def add_far(group, src_ref, dst_ref, v_ref, inner_ref, outer_ref, out_ref):
    rhs = v_ref.shape[1]
    panels = src_ref.shape[0]
    prank = inner_ref.shape[0] // panels
    shape = (group * rhs, group * prank)
    of_row = lax.div(lax.broadcasted_iota(jnp.int32, shape, 0), rhs)
    of_lane = lax.div(lax.broadcasted_iota(jnp.int32, shape, 1), prank)
    same = of_row == of_lane
    for start in range(0, panels, group):
        v = jnp.concatenate([v_ref[src_ref[start + g]] for g in range(group)], axis=0)
        part = pl.ds(start * prank, group * prank)
        half = lax.dot_general(v, inner_ref[part, :], NT, preferred_element_type=F32)
        half = jnp.where(same, half, 0.0).astype(BF16)
        prod = lax.dot_general(half, outer_ref[part, :], NN, preferred_element_type=F32)
        for g in range(group):
            out_ref[dst_ref[start + g]] += prod[g * rhs : (g + 1) * rhs]


def far_kernel(group, src_ref, dst_ref, v_ref, inner_ref, outer_ref, out_ref):
    out_ref[...] = jnp.zeros_like(out_ref)
    add_far(group, src_ref, dst_ref, v_ref, inner_ref, outer_ref, out_ref)


def far_products(v, src, dst, inner, outer, out_blocks):
    _, rhs, width = v.shape
    smem = pl.BlockSpec(memory_space=pltpu.SMEM)
    vmem = pl.BlockSpec(memory_space=pltpu.VMEM)
    return pl.pallas_call(
        functools.partial(far_kernel, GROUP),
        out_shape=jax.ShapeDtypeStruct((out_blocks, rhs, width), F32),
        in_specs=[smem] * 2 + [vmem] * 3,
        out_specs=vmem,
        compiler_params=pltpu.CompilerParams(vmem_limit_bytes=VMEM_LIMIT),
        cost_estimate=pl.CostEstimate(
            flops=4 * rhs * width * inner.shape[0],
            bytes_accessed=2 * inner.size,
            transcendentals=0,
        ),
        name="far_transposed",
    )(src, dst, v, inner, outer)


def eliminate(systems, block=8):
    size, lanes = systems[0].shape
    parts = [[s[t : t + 8, :] for t in range(0, size, 8)] for s in systems]
    sub = lax.broadcasted_iota(jnp.int32, (8, lanes), 0)
    every = range(block)
    for k in range(0, size, block):
        home, offset = k // 8, k % 8
        for n, part in enumerate(parts):
            cols = [[jnp.broadcast_to(p[:, k + j : k + j + 1], p.shape) for p in part] for j in every]
            head = part[home]
            rows = [jnp.broadcast_to(head[offset + i : offset + i + 1, :], head.shape) for i in every]
            small = [
                [jnp.broadcast_to(cols[j][home][offset + i : offset + i + 1, :], head.shape) for j in every]
                for i in every
            ]
            for p in every:
                inverse = 1.0 / small[p][p]
                rows[p] = rows[p] * inverse
                for j in range(p + 1, block):
                    small[p][j] = small[p][j] * inverse
                for i in every:
                    if i != p:
                        factor = small[i][p]
                        rows[i] = rows[i] - factor * rows[p]
                        for j in range(p + 1, block):
                            small[i][j] = small[i][j] - factor * small[p][j]
            for t in range(len(part)):
                value = part[t]
                for j in every:
                    value = value - cols[j][t] * rows[j]
                part[t] = value
            for i in every:
                part[home] = jnp.where(sub == offset + i, rows[i], part[home])
    return [jnp.concatenate(part, axis=0)[:, size:] for part in parts]


def symmetric(matrix):
    return 0.5 * (matrix + matrix.T)


def call(kernel, outs, name, operands, after=(), limit=VMEM_LIMIT):
    vmem = pl.BlockSpec(memory_space=pltpu.VMEM)

    def body(*refs):
        kernel(*refs[len(after) :])

    return pl.pallas_call(
        body,
        out_shape=[jax.ShapeDtypeStruct(shape, dtype) for shape, dtype in outs],
        in_specs=[pl.BlockSpec(memory_space=pl.ANY)] * len(after) + [vmem] * len(operands),
        out_specs=[vmem] * len(outs),
        compiler_params=pltpu.CompilerParams(vmem_limit_bytes=limit),
        name=name,
    )(*after, *operands)


def pack(direc, packed_ref):
    blocks, _, width = packed_ref.shape
    for b in range(blocks):
        packed_ref[b] = direc[:, b * width : (b + 1) * width].astype(BF16)


def project_kernel(rhs_hbm, factor_hbm, out_ref, rhs, factor, arrived):
    parts = arrived.shape[0] - 1
    ranks = factor.shape[0] // parts
    copies = [pltpu.make_async_copy(rhs_hbm, rhs, arrived.at[parts])]
    for p in range(parts):
        part = pl.ds(p * ranks, ranks)
        copies.append(
            pltpu.make_async_copy(factor_hbm.at[part], factor.at[part], arrived.at[p])
        )
    for copy in copies:
        copy.start()
    copies[0].wait()
    resid = rhs[...]
    done = []
    for p in range(parts):
        copies[1 + p].wait()
        done.append(exact(factor[p * ranks : (p + 1) * ranks], resid, NT).T)
    to_pieces(jnp.concatenate(done, axis=1), out_ref)


def project(shape, rhs, factor):
    parts = 2
    return pl.pallas_call(
        project_kernel,
        out_shape=jax.ShapeDtypeStruct(shape, F32),
        in_specs=[pl.BlockSpec(memory_space=pltpu.HBM)] * 2,
        out_specs=pl.BlockSpec(memory_space=pltpu.VMEM),
        scratch_shapes=[
            pltpu.VMEM(rhs.shape, F32),
            pltpu.VMEM(factor.shape, F32),
            pltpu.SemaphoreType.DMA((parts + 1,)),
        ],
        compiler_params=pltpu.CompilerParams(vmem_limit_bytes=PROJECT_LIMIT),
        name="project",
    )(rhs, factor)


def stage_kernel(*refs):
    sources, held, arrived = refs[: len(refs) // 2], refs[len(refs) // 2 : -1], refs[-1]
    copies = [
        pltpu.make_async_copy(source, target, arrived.at[index])
        for index, (source, target) in enumerate(zip(sources, held))
    ]
    for copy in copies:
        copy.start()
    for copy in copies:
        copy.wait()


def stage(operands):
    return pl.pallas_call(
        stage_kernel,
        out_shape=[jax.ShapeDtypeStruct(value.shape, value.dtype) for value in operands],
        in_specs=[pl.BlockSpec(memory_space=pltpu.HBM)] * len(operands),
        out_specs=[pl.BlockSpec(memory_space=pltpu.VMEM)] * len(operands),
        scratch_shapes=[pltpu.SemaphoreType.DMA((len(operands),))],
        compiler_params=pltpu.CompilerParams(vmem_limit_bytes=VMEM_LIMIT),
        cost_estimate=pl.CostEstimate(flops=0, bytes_accessed=2**24, transcendentals=0),
        name="stage",
    )(*operands)


def begin_kernel(rhs, weight, factor, proj_ref, direc_ref, packed_ref):
    proj = from_pieces(proj_ref)
    direc = rhs[...] + exact(proj * weight[...], factor[...], NN)
    direc_ref[...] = direc
    pack(direc, packed_ref)


def image_of(self_term, direc, terms):
    both = terms[0][...] + terms[1][...] + terms[2][...] + terms[3][...]
    return self_term * direc + jnp.concatenate([both[b] for b in range(both.shape[0])], axis=1)


def copy_kernel(value_ref, out_ref):
    out_ref[...] = value_ref[...]


def fold_kernel(*refs):
    paths = len(refs) // 4
    own, got, keep, send = (refs[paths * index : paths * (index + 1)] for index in range(4))
    for p in range(paths):
        half = own[p].shape[0] // 2
        keep[p][...] = own[p][:half] + got[p][:half]
        send[p][...] = own[p][half:] + got[p][half:]


def join_kernel(transposed_ref, *refs):
    paths = len(refs) // 2 - 2
    keep, send, col_keep, col_send = refs[-4:]
    for p in range(paths):
        own, got = refs[p], refs[paths + p]
        half = own.shape[0] // 2
        part = pl.ds(p * half, half)
        keep[part] = own[:half] + got[:half]
        send[part] = own[half:] + got[half:]
    half = col_keep.shape[0]
    col_keep[...] = transposed_ref[:half]
    col_send[...] = transposed_ref[half:]


def inner_kernel(self_term, rhs, factor, direc_ref, *refs):
    terms, (image_ref, out_ref) = refs[:-2], refs[-2:]
    direc = direc_ref[...]
    image = image_of(self_term[...], direc, terms)
    image_ref[...] = image
    resid = rhs[...]
    count = resid.shape[0]
    stack = jnp.concatenate([direc, resid, image], axis=0)
    against = exact(stack, image, NT)
    own = exact(resid, resid, NT)
    pairs = jnp.concatenate(
        [against[:count], against[count : 2 * count], against[2 * count :], own], axis=1
    )
    to_pieces(jnp.concatenate([exact(image, factor[...], NT), pairs], axis=1), out_ref)


def advance_kernel(
    weight_ref,
    factor,
    rhs,
    sums_ref,
    proj_ref,
    direc_ref,
    image_ref,
    solution_ref,
    resid_ref,
    next_ref,
    packed_ref,
    rho_ref,
):
    count = rho_ref.shape[0]
    weight, proj, sums = weight_ref[...], from_pieces(proj_ref), from_pieces(sums_ref)
    rank = proj.shape[1]
    image_proj = sums[:, :rank]
    gram, cross, square, own = (
        sums[:, rank + count * index : rank + count * (index + 1)] for index in range(4)
    )
    rho = own + exact(proj * weight, proj, NT)
    unit = (
        lax.broadcasted_iota(jnp.int32, (count, count), 0)
        == lax.broadcasted_iota(jnp.int32, (count, count), 1)
    ).astype(F32)
    alpha, inverse = eliminate(
        [
            jnp.concatenate([symmetric(gram), rho], axis=1),
            jnp.concatenate([symmetric(rho), unit], axis=1),
        ]
    )
    alpha_t = alpha.T
    proj = proj - exact(alpha_t, image_proj, NN)
    mixed = exact(cross, alpha, NN)
    new = own - mixed - mixed.T + exact(exact(alpha_t, square, NN), alpha, NN)
    new = new + exact(proj * weight, proj, NT)
    beta = exact(inverse, new, NN)
    direc = direc_ref[...]
    resid = rhs[...] - exact(alpha_t, image_ref[...], NN)
    after = resid + exact(proj * weight, factor[...], NN) + exact(beta.T, direc, NN)
    pack(after, packed_ref)
    solution_ref[...] = exact(alpha_t, direc, NN)
    resid_ref[...] = resid
    next_ref[...] = after
    rho_ref[...] = new


def last_image_kernel(self_term, direc_ref, *refs):
    terms, (image_ref, gram_ref) = refs[:-2], refs[-2:]
    direc = direc_ref[...]
    image = image_of(self_term[...], direc, terms)
    image_ref[...] = image
    gram = exact(direc, image, NT)
    half = gram.shape[0] // 2
    gram_ref[...] = jnp.concatenate([gram[:half], gram[half:]], axis=1)


def finish_kernel(
    gram_ref, rho_ref, solution_ref, resid_ref, direc_ref, image_ref, out_ref, left_ref
):
    count = rho_ref.shape[0]
    gram = gram_ref[0]
    for index in range(1, gram_ref.shape[0]):
        gram = gram + gram_ref[index]
    gram = jnp.concatenate([gram[:, :count], gram[:, count:]], axis=0)
    (alpha,) = eliminate([jnp.concatenate([symmetric(gram), rho_ref[...]], axis=1)])
    alpha_t = alpha.T
    out_ref[...] = solution_ref[...] + exact(alpha_t, direc_ref[...], NN)
    left_ref[...] = resid_ref[...] - exact(alpha_t, image_ref[...], NN)


def local(
    rhs,
    self_term,
    near_tiles,
    near_rows,
    near_cols,
    near_counts,
    far_left,
    far_right,
    far_rows,
    far_cols,
    nys_factor,
    nys_weight,
):
    width = near_tiles.shape[1]
    count_rhs, columns = rhs.shape
    blocks = columns // width
    n_row, n_col = lax.axis_size("row"), lax.axis_size("col")
    grid_row, grid_col = lax.axis_index("row"), lax.axis_index("col")
    count = near_counts[grid_row * n_col + grid_col]
    rank = nys_factor.shape[0]
    self_row = self_term.reshape(1, columns)
    weight = nys_weight.reshape(1, rank)
    prank = far_left.shape[2]
    left = far_left.transpose(0, 2, 1).reshape(-1, width)
    right = far_right.transpose(0, 2, 1).reshape(-1, width)

    col_masks, row_masks = masks_of("col"), masks_of("row")
    gather_col, gather_row = col_masks[::-1], row_masks[::-1]
    path_a = col_masks[-2::-1] + col_masks[-1:]
    path_b = col_masks
    scatter_row = row_masks

    def relative(ids, me):
        return jnp.bitwise_xor(ids // blocks, me), ids % blocks

    def gathered(ids, me, masks):
        device, block = relative(ids, me)
        return place(device, masks[::-1]) * blocks + block

    def scattered_col(ids):
        device, block = relative(ids, grid_col)
        path = jnp.where(block % 2 == 0, place(device, path_a), place(device, path_b))
        return block * n_col + path

    def scattered_row(ids):
        device, block = relative(ids, grid_row)
        return place(device, scatter_row) * blocks + block

    row_src = gathered(near_rows, grid_col, gather_col)
    col_src = gathered(near_cols, grid_row, gather_row)
    far_row_src = gathered(far_rows, grid_col, gather_col)
    far_col_src = gathered(far_cols, grid_row, gather_row)
    row_dst, far_row_dst = scattered_col(near_rows), scattered_col(far_rows)
    col_dst, far_col_dst = scattered_row(near_cols), scattered_row(far_cols)

    def operate(packed, tiles, first):
        col_side = row_side = packed
        for mask in gather_row:
            col_side = jnp.concatenate([col_side, swap(col_side, "row", mask)], axis=0)
        for mask in gather_col[:-1]:
            row_side = jnp.concatenate([row_side, swap(row_side, "col", mask)], axis=0)
        near = (count, col_src, row_dst)
        forward, *streamed = near_products(
            True, col_side, tiles, *near, part=(0, 2), out_blocks=n_col * blocks, stream=first
        )
        held = streamed[0] if first else tiles
        (row_side,) = call(
            copy_kernel, [(row_side.shape, BF16)], "gathered", [row_side], [forward]
        )
        (forward,) = near_products(
            True, col_side, held, *near, part=(1, 2), start=forward, after=[row_side],
            far=(far_col_src, far_row_dst, right, left),
        )
        other_side = swap(row_side, "col", gather_col[-1])
        row_side = jnp.concatenate([row_side, other_side], axis=0)

        half = n_col // 2
        sends = [forward[b * n_col + half : (b + 1) * n_col] for b in range(blocks)]
        paths = [path_a if b % 2 == 0 else path_b for b in range(blocks)]
        got = [swap(sends[b], "col", paths[b][0]) for b in range(blocks)]
        transposed = far_products(
            row_side, far_row_src, far_col_dst, left, right, n_row * blocks
        )
        own = [forward[b * n_col : b * n_col + half] for b in range(blocks)]
        for step in range(1, len(col_masks) - 1):
            size = (own[0].shape[0] // 2, count_rhs, width)
            folded = call(
                fold_kernel, [(size, F32)] * (2 * blocks), "fold", [*own, *got], [transposed]
            )
            own = folded[:blocks]
            got = [swap(folded[blocks + b], "col", paths[b][step]) for b in range(blocks)]
            if step == 1:
                (transposed,) = near_products(
                    False, row_side, held, count, row_src, col_dst, start=transposed,
                    after=[folded[blocks]],
                )
        size = (own[0].shape[0] // 2 * blocks, count_rhs, width)
        col_size = (n_row * blocks // 2, count_rhs, width)
        own, send, col_own, col_send = call(
            join_kernel, [(size, F32)] * 2 + [(col_size, F32)] * 2, "join", [transposed, *own, *got]
        )
        row_terms = (own, swap(send, "col", col_masks[-1]))
        for step, mask in enumerate(scatter_row):
            if step:
                transposed = col_own + col_got
                half = transposed.shape[0] // 2
                col_own, col_send = transposed[:half], transposed[half:]
            col_got = swap(col_send, "row", mask)
        col_terms = (col_own, col_got)
        return [*row_terms, *col_terms], held

    devices = n_row * n_col
    full, packs = (count_rhs, columns), (blocks, count_rhs, width)
    shape_of = lambda wanted: pieces_shape(count_rhs, wanted, devices)
    partial = project(shape_of(rank), rhs, nys_factor)
    count = count.reshape(1)
    rhs, nys_factor, weight, self_row = stage([rhs, nys_factor, weight, self_row])
    proj = spread_sum(partial)
    direc, packed = call(
        begin_kernel, [(full, F32), (packs, BF16)], "begin", [rhs, weight, nys_factor, proj]
    )
    terms, tiles = operate(packed, near_tiles, True)
    image, partial = call(
        inner_kernel, [(full, F32), (shape_of(rank + 4 * count_rhs), F32)], "inner",
        [self_row, rhs, nys_factor, direc, *terms],
    )
    sums = spread_sum(partial)
    solution, residual, direc, packed, rho = call(
        advance_kernel,
        [(full, F32), (full, F32), (full, F32), (packs, BF16), ((count_rhs, count_rhs), F32)],
        "advance", [weight, nys_factor, rhs, sums, proj, direc, image],
    )
    terms, _ = operate(packed, tiles, False)
    image, partial = call(
        last_image_kernel, [(full, F32), ((count_rhs // 2, 2 * count_rhs), F32)], "last_image",
        [self_row, direc, *terms],
    )
    for mask in row_masks:
        partial = partial + swap(partial, "row", mask)
    gram = lax.all_to_all(
        jnp.broadcast_to(partial, (n_col, *partial.shape)), "col", 0, 0, tiled=True
    )
    return tuple(
        call(
            finish_kernel, [(full, F32), (full, F32)], "finish",
            [gram, rho, solution, residual, direc, image],
        )
    )


def solution(mesh):
    in_specs = (
        P(None, ("row", "col")),
        P(("row", "col")),
        P(("row", "col"), None, None),
        P(("row", "col")),
        P(("row", "col")),
        P(),
        P(("row", "col"), None, None),
        P(("row", "col"), None, None),
        P(("row", "col")),
        P(("row", "col")),
        P(None, ("row", "col")),
        P(),
    )
    out_specs = (P(None, ("row", "col")), P(None, ("row", "col")))
    return jax.shard_map(local, mesh=mesh, in_specs=in_specs, out_specs=out_specs, check_vma=False)
```

```python
import jax
import jax.numpy as jnp
from jax import lax
from jax.experimental import pallas as pl
from jax.experimental.pallas import tpu as pltpu
from jax.sharding import PartitionSpec as P

F32 = jnp.float32
BF16 = jnp.bfloat16
NN = (((1,), (0,)), ((), ()))
NT = (((1,), (1,)), ((), ()))
VMEM_LIMIT = 18 * 2**20
PROJECT_LIMIT = 62 * 2**20
STREAM_LIMIT = 36 * 2**20


def exact(left, right, dims):
    return lax.dot_general(
        left, right, dims, precision=lax.Precision.HIGHEST, preferred_element_type=F32
    )


def masks_of(axis):
    return [2**bit for bit in range(lax.axis_size(axis).bit_length() - 1)]


def swap(value, axis, mask):
    pairs = [(source, source ^ mask) for source in range(lax.axis_size(axis))]
    return lax.ppermute(value, axis, pairs)


def place(device, masks):
    spot = jnp.zeros_like(device)
    for mask in masks:
        spot = spot * 2 + (jnp.bitwise_and(device, mask) != 0).astype(jnp.int32)
    return spot


def pieces_shape(rows, columns, devices):
    return (devices, 2 * rows // devices, columns // 2)


def to_pieces(value, pieces_ref):
    pieces, depth, width = pieces_ref.shape
    for piece in range(pieces):
        row, half = piece // 2 * depth, piece % 2 * width
        pieces_ref[piece] = value[row : row + depth, half : half + width]


def from_pieces(pieces_ref):
    pieces = pieces_ref.shape[0]
    halves = [[pieces_ref[p] for p in range(side, pieces, 2)] for side in (0, 1)]
    return jnp.concatenate([jnp.concatenate(half, axis=0) for half in halves], axis=1)


def total_kernel(got_ref, out_ref):
    total = got_ref[0]
    for piece in range(1, got_ref.shape[0]):
        total = total + got_ref[piece]
    for piece in range(got_ref.shape[0]):
        out_ref[piece] = total


def spread_sum(pieces):
    axes = ("row", "col")
    got = lax.all_to_all(pieces, axes, 0, 0, tiled=True)
    (same,) = call(total_kernel, [(pieces.shape, F32)], "total", [got])
    return lax.all_to_all(same, axes, 0, 0, tiled=True)


def near_kernel(forward, chunk, stream, part, count_ref, src_ref, dst_ref, v_ref, tiles_ref, *refs):
    count = count_ref[0]
    chunks = lax.div(count + (chunk - 1), chunk)
    slots = tiles_ref.shape[0]
    if stream:
        out_ref, held_ref, arrived = refs

        def fetch(index):
            part = pl.ds(index * chunk, chunk)
            return pltpu.make_async_copy(
                tiles_ref.at[part], held_ref.at[part], arrived.at[index]
            )

        for index in range(slots // chunk):

            @pl.when(index < chunks)
            def _():
                fetch(index).start()

    else:
        out_ref, held_ref = refs[-1], tiles_ref
    out_ref[...] = jnp.zeros_like(out_ref) if stream or len(refs) == 1 else refs[0][...]

    first, last = (lax.min(chunks, slots // chunk * (part[0] + end) // part[1]) for end in (0, 1))

    def near(index, carry):
        if stream:
            fetch(index).wait()
        for s in range(chunk):
            tile = index * chunk + s
            v = v_ref[src_ref[tile]]
            v = jnp.where(tile < count, v, jnp.zeros_like(v))
            out_ref[dst_ref[tile]] += lax.dot_general(
                v, held_ref[tile], NT if forward else NN, preferred_element_type=F32
            )
        return carry

    lax.fori_loop(first, last, near, 0)
    if stream:

        def rest(index, carry):
            fetch(index).wait()
            return carry

        lax.fori_loop(last, chunks, rest, 0)


def near_products(
    forward, v, tiles, count, src, dst, part=(0, 1), out_blocks=None, start=None, stream=False, after=()
):
    slots, width, _ = tiles.shape
    rhs = v.shape[1]
    chunk = 32

    def body(*refs):
        near_kernel(forward, chunk, stream, part, *refs[len(after) :])

    extra = [] if start is None else [start]
    total = jax.ShapeDtypeStruct((out_blocks, rhs, width) if start is None else start.shape, F32)
    smem = pl.BlockSpec(memory_space=pltpu.SMEM)
    vmem = pl.BlockSpec(memory_space=pltpu.VMEM)
    hbm = pl.BlockSpec(memory_space=pltpu.HBM)
    return pl.pallas_call(
        body,
        out_shape=[total, jax.ShapeDtypeStruct(tiles.shape, tiles.dtype)] if stream else [total],
        in_specs=[pl.BlockSpec(memory_space=pl.ANY)] * len(after)
        + [smem] * 3
        + [vmem]
        + [hbm if stream else vmem]
        + [vmem] * len(extra),
        out_specs=[vmem, vmem] if stream else [vmem],
        scratch_shapes=[pltpu.SemaphoreType.DMA((slots // chunk,))] if stream else [],
        compiler_params=pltpu.CompilerParams(vmem_limit_bytes=STREAM_LIMIT if stream else VMEM_LIMIT),
        cost_estimate=pl.CostEstimate(
            flops=4 * slots * rhs * width * width,
            bytes_accessed=2 * slots * width * width,
            transcendentals=0,
        ),
        name="near_forward" if forward else "near_transposed",
    )(*after, count, src, dst, v, tiles, *extra)


def far_kernel(group, src_ref, dst_ref, v_ref, inner_ref, outer_ref, *refs):
    rhs = v_ref.shape[1]
    out_ref = refs[-1]
    if len(refs) == 2:
        out_ref[...] = refs[0][...]
    else:
        out_ref[...] = jnp.zeros_like(out_ref)
    panels = src_ref.shape[0]
    prank = inner_ref.shape[0] // panels
    shape = (group * rhs, group * prank)
    of_row = lax.div(lax.broadcasted_iota(jnp.int32, shape, 0), rhs)
    of_lane = lax.div(lax.broadcasted_iota(jnp.int32, shape, 1), prank)
    same = of_row == of_lane
    for start in range(0, panels, group):
        v = jnp.concatenate([v_ref[src_ref[start + g]] for g in range(group)], axis=0)
        part = pl.ds(start * prank, group * prank)
        half = lax.dot_general(v, inner_ref[part, :], NT, preferred_element_type=F32)
        half = jnp.where(same, half, 0.0).astype(BF16)
        prod = lax.dot_general(half, outer_ref[part, :], NN, preferred_element_type=F32)
        for g in range(group):
            out_ref[dst_ref[start + g]] += prod[g * rhs : (g + 1) * rhs]


def far_products(forward, v, src, dst, inner, outer, out_blocks=None, start=None, after=()):
    panels = src.shape[0]
    _, rhs, width = v.shape
    smem = pl.BlockSpec(memory_space=pltpu.SMEM)
    vmem = pl.BlockSpec(memory_space=pltpu.VMEM)
    extra = [] if start is None else [start]
    total = (out_blocks, rhs, width) if start is None else start.shape

    def body(*refs):
        far_kernel(8, *refs[len(after) :])

    return pl.pallas_call(
        body,
        out_shape=jax.ShapeDtypeStruct(total, F32),
        in_specs=[pl.BlockSpec(memory_space=pl.ANY)] * len(after)
        + [smem] * 2
        + [vmem] * (3 + len(extra)),
        out_specs=vmem,
        compiler_params=pltpu.CompilerParams(vmem_limit_bytes=VMEM_LIMIT),
        cost_estimate=pl.CostEstimate(
            flops=2 * panels * rhs * width * inner.shape[0] // panels,
            bytes_accessed=2 * inner.size,
            transcendentals=0,
        ),
        name="far_forward" if forward else "far_transposed",
    )(*after, src, dst, v, inner, outer, *extra)


def eliminate(systems, block=8):
    size, lanes = systems[0].shape
    parts = [[s[t : t + 8, :] for t in range(0, size, 8)] for s in systems]
    sub = lax.broadcasted_iota(jnp.int32, (8, lanes), 0)
    every = range(block)
    for k in range(0, size, block):
        home, offset = k // 8, k % 8
        for n, part in enumerate(parts):
            cols = [[jnp.broadcast_to(p[:, k + j : k + j + 1], p.shape) for p in part] for j in every]
            head = part[home]
            rows = [jnp.broadcast_to(head[offset + i : offset + i + 1, :], head.shape) for i in every]
            small = [
                [jnp.broadcast_to(cols[j][home][offset + i : offset + i + 1, :], head.shape) for j in every]
                for i in every
            ]
            for p in every:
                inverse = 1.0 / small[p][p]
                rows[p] = rows[p] * inverse
                for j in range(p + 1, block):
                    small[p][j] = small[p][j] * inverse
                for i in every:
                    if i != p:
                        factor = small[i][p]
                        rows[i] = rows[i] - factor * rows[p]
                        for j in range(p + 1, block):
                            small[i][j] = small[i][j] - factor * small[p][j]
            for t in range(len(part)):
                value = part[t]
                for j in every:
                    value = value - cols[j][t] * rows[j]
                part[t] = value
            for i in every:
                part[home] = jnp.where(sub == offset + i, rows[i], part[home])
    return [jnp.concatenate(part, axis=0)[:, size:] for part in parts]


def symmetric(matrix):
    return 0.5 * (matrix + matrix.T)


def call(kernel, outs, name, operands, after=(), limit=VMEM_LIMIT):
    vmem = pl.BlockSpec(memory_space=pltpu.VMEM)

    def body(*refs):
        kernel(*refs[len(after) :])

    return pl.pallas_call(
        body,
        out_shape=[jax.ShapeDtypeStruct(shape, dtype) for shape, dtype in outs],
        in_specs=[pl.BlockSpec(memory_space=pl.ANY)] * len(after) + [vmem] * len(operands),
        out_specs=[vmem] * len(outs),
        compiler_params=pltpu.CompilerParams(vmem_limit_bytes=limit),
        name=name,
    )(*after, *operands)


def pack(direc, packed_ref):
    blocks, _, width = packed_ref.shape
    for b in range(blocks):
        packed_ref[b] = direc[:, b * width : (b + 1) * width].astype(BF16)


def project_kernel(rhs_hbm, factor_hbm, out_ref, rhs, factor, arrived):
    parts = arrived.shape[0] - 1
    ranks = factor.shape[0] // parts
    copies = [pltpu.make_async_copy(rhs_hbm, rhs, arrived.at[parts])]
    for p in range(parts):
        part = pl.ds(p * ranks, ranks)
        copies.append(
            pltpu.make_async_copy(factor_hbm.at[part], factor.at[part], arrived.at[p])
        )
    for copy in copies:
        copy.start()
    copies[0].wait()
    resid = rhs[...]
    done = []
    for p in range(parts):
        copies[1 + p].wait()
        done.append(exact(factor[p * ranks : (p + 1) * ranks], resid, NT).T)
    to_pieces(jnp.concatenate(done, axis=1), out_ref)


def project(shape, rhs, factor):
    parts = 2
    return pl.pallas_call(
        project_kernel,
        out_shape=jax.ShapeDtypeStruct(shape, F32),
        in_specs=[pl.BlockSpec(memory_space=pltpu.HBM)] * 2,
        out_specs=pl.BlockSpec(memory_space=pltpu.VMEM),
        scratch_shapes=[
            pltpu.VMEM(rhs.shape, F32),
            pltpu.VMEM(factor.shape, F32),
            pltpu.SemaphoreType.DMA((parts + 1,)),
        ],
        compiler_params=pltpu.CompilerParams(vmem_limit_bytes=PROJECT_LIMIT),
        name="project",
    )(rhs, factor)


def stage_kernel(*refs):
    sources, held, arrived = refs[: len(refs) // 2], refs[len(refs) // 2 : -1], refs[-1]
    copies = [
        pltpu.make_async_copy(source, target, arrived.at[index])
        for index, (source, target) in enumerate(zip(sources, held))
    ]
    for copy in copies:
        copy.start()
    for copy in copies:
        copy.wait()


def stage(operands):
    return pl.pallas_call(
        stage_kernel,
        out_shape=[jax.ShapeDtypeStruct(value.shape, value.dtype) for value in operands],
        in_specs=[pl.BlockSpec(memory_space=pltpu.HBM)] * len(operands),
        out_specs=[pl.BlockSpec(memory_space=pltpu.VMEM)] * len(operands),
        scratch_shapes=[pltpu.SemaphoreType.DMA((len(operands),))],
        compiler_params=pltpu.CompilerParams(vmem_limit_bytes=VMEM_LIMIT),
        cost_estimate=pl.CostEstimate(flops=0, bytes_accessed=2**24, transcendentals=0),
        name="stage",
    )(*operands)


def begin_kernel(rhs, weight, factor, proj_ref, direc_ref, packed_ref):
    proj = from_pieces(proj_ref)
    direc = rhs[...] + exact(proj * weight[...], factor[...], NN)
    direc_ref[...] = direc
    pack(direc, packed_ref)


def image_of(self_term, direc, terms):
    both = terms[0][...] + terms[1][...] + terms[2][...] + terms[3][...]
    return self_term * direc + jnp.concatenate([both[b] for b in range(both.shape[0])], axis=1)


def copy_kernel(value_ref, out_ref):
    out_ref[...] = value_ref[...]


def fold_kernel(*refs):
    paths = len(refs) // 4
    own, got, keep, send = (refs[paths * index : paths * (index + 1)] for index in range(4))
    for p in range(paths):
        half = own[p].shape[0] // 2
        keep[p][...] = own[p][:half] + got[p][:half]
        send[p][...] = own[p][half:] + got[p][half:]


def join_kernel(transposed_ref, *refs):
    paths = len(refs) // 2 - 2
    keep, send, col_keep, col_send = refs[-4:]
    for p in range(paths):
        own, got = refs[p], refs[paths + p]
        half = own.shape[0] // 2
        part = pl.ds(p * half, half)
        keep[part] = own[:half] + got[:half]
        send[part] = own[half:] + got[half:]
    half = col_keep.shape[0]
    col_keep[...] = transposed_ref[:half]
    col_send[...] = transposed_ref[half:]


def inner_kernel(self_term, rhs, factor, direc_ref, *refs):
    terms, (image_ref, out_ref) = refs[:-2], refs[-2:]
    direc = direc_ref[...]
    image = image_of(self_term[...], direc, terms)
    image_ref[...] = image
    resid = rhs[...]
    count = resid.shape[0]
    stack = jnp.concatenate([direc, resid, image], axis=0)
    against = exact(stack, image, NT)
    own = exact(resid, resid, NT)
    pairs = jnp.concatenate(
        [against[:count], against[count : 2 * count], against[2 * count :], own], axis=1
    )
    to_pieces(jnp.concatenate([exact(image, factor[...], NT), pairs], axis=1), out_ref)


def advance_kernel(
    weight_ref,
    factor,
    rhs,
    sums_ref,
    proj_ref,
    direc_ref,
    image_ref,
    solution_ref,
    resid_ref,
    next_ref,
    packed_ref,
    rho_ref,
):
    count = rho_ref.shape[0]
    weight, proj, sums = weight_ref[...], from_pieces(proj_ref), from_pieces(sums_ref)
    rank = proj.shape[1]
    image_proj = sums[:, :rank]
    gram, cross, square, own = (
        sums[:, rank + count * index : rank + count * (index + 1)] for index in range(4)
    )
    rho = own + exact(proj * weight, proj, NT)
    unit = (
        lax.broadcasted_iota(jnp.int32, (count, count), 0)
        == lax.broadcasted_iota(jnp.int32, (count, count), 1)
    ).astype(F32)
    alpha, inverse = eliminate(
        [
            jnp.concatenate([symmetric(gram), rho], axis=1),
            jnp.concatenate([symmetric(rho), unit], axis=1),
        ]
    )
    alpha_t = alpha.T
    proj = proj - exact(alpha_t, image_proj, NN)
    mixed = exact(cross, alpha, NN)
    new = own - mixed - mixed.T + exact(exact(alpha_t, square, NN), alpha, NN)
    new = new + exact(proj * weight, proj, NT)
    beta = exact(inverse, new, NN)
    direc = direc_ref[...]
    resid = rhs[...] - exact(alpha_t, image_ref[...], NN)
    after = resid + exact(proj * weight, factor[...], NN) + exact(beta.T, direc, NN)
    pack(after, packed_ref)
    solution_ref[...] = exact(alpha_t, direc, NN)
    resid_ref[...] = resid
    next_ref[...] = after
    rho_ref[...] = new


def last_image_kernel(self_term, direc_ref, *refs):
    terms, (image_ref, gram_ref) = refs[:-2], refs[-2:]
    direc = direc_ref[...]
    image = image_of(self_term[...], direc, terms)
    image_ref[...] = image
    gram = exact(direc, image, NT)
    half = gram.shape[0] // 2
    gram_ref[...] = jnp.concatenate([gram[:half], gram[half:]], axis=1)


def finish_kernel(
    gram_ref, rho_ref, solution_ref, resid_ref, direc_ref, image_ref, out_ref, left_ref
):
    count = rho_ref.shape[0]
    gram = gram_ref[0]
    for index in range(1, gram_ref.shape[0]):
        gram = gram + gram_ref[index]
    gram = jnp.concatenate([gram[:, :count], gram[:, count:]], axis=0)
    (alpha,) = eliminate([jnp.concatenate([symmetric(gram), rho_ref[...]], axis=1)])
    alpha_t = alpha.T
    out_ref[...] = solution_ref[...] + exact(alpha_t, direc_ref[...], NN)
    left_ref[...] = resid_ref[...] - exact(alpha_t, image_ref[...], NN)


def local(
    rhs,
    self_term,
    near_tiles,
    near_rows,
    near_cols,
    near_counts,
    far_left,
    far_right,
    far_rows,
    far_cols,
    nys_factor,
    nys_weight,
):
    width = near_tiles.shape[1]
    count_rhs, columns = rhs.shape
    blocks = columns // width
    n_row, n_col = lax.axis_size("row"), lax.axis_size("col")
    grid_row, grid_col = lax.axis_index("row"), lax.axis_index("col")
    count = near_counts[grid_row * n_col + grid_col]
    rank = nys_factor.shape[0]
    self_row = self_term.reshape(1, columns)
    weight = nys_weight.reshape(1, rank)
    prank = far_left.shape[2]
    left = far_left.transpose(0, 2, 1).reshape(-1, width)
    right = far_right.transpose(0, 2, 1).reshape(-1, width)

    col_masks, row_masks = masks_of("col"), masks_of("row")
    gather_col, gather_row = col_masks[::-1], row_masks[::-1]
    path_a = col_masks[-2::-1] + col_masks[-1:]
    path_b = col_masks
    scatter_row = row_masks

    def relative(ids, me):
        return jnp.bitwise_xor(ids // blocks, me), ids % blocks

    def gathered(ids, me, masks):
        device, block = relative(ids, me)
        return place(device, masks[::-1]) * blocks + block

    def scattered_col(ids):
        device, block = relative(ids, grid_col)
        path = jnp.where(block % 2 == 0, place(device, path_a), place(device, path_b))
        return block * n_col + path

    def scattered_row(ids):
        device, block = relative(ids, grid_row)
        return place(device, scatter_row) * blocks + block

    row_src = gathered(near_rows, grid_col, gather_col)
    col_src = gathered(near_cols, grid_row, gather_row)
    far_row_src = gathered(far_rows, grid_col, gather_col)
    far_col_src = gathered(far_cols, grid_row, gather_row)
    row_dst, far_row_dst = scattered_col(near_rows), scattered_col(far_rows)
    col_dst, far_col_dst = scattered_row(near_cols), scattered_row(far_cols)

    def operate(packed, tiles, first):
        col_side = row_side = packed
        for mask in gather_row:
            col_side = jnp.concatenate([col_side, swap(col_side, "row", mask)], axis=0)
        for mask in gather_col[:-1]:
            row_side = jnp.concatenate([row_side, swap(row_side, "col", mask)], axis=0)
        near = (count, col_src, row_dst)
        forward, *streamed = near_products(
            True, col_side, tiles, *near, part=(0, 2), out_blocks=n_col * blocks, stream=first
        )
        held = streamed[0] if first else tiles
        (row_side,) = call(
            copy_kernel, [(row_side.shape, BF16)], "gathered", [row_side], [forward]
        )
        (forward,) = near_products(
            True, col_side, held, *near, part=(1, 2), start=forward, after=[row_side]
        )
        other_side = swap(row_side, "col", gather_col[-1])
        forward = far_products(
            True, col_side, far_col_src, far_row_dst, right, left, start=forward
        )
        row_side = jnp.concatenate([row_side, other_side], axis=0)

        half = n_col // 2
        sends = [forward[b * n_col + half : (b + 1) * n_col] for b in range(blocks)]
        paths = [path_a if b % 2 == 0 else path_b for b in range(blocks)]
        got = [swap(sends[b], "col", paths[b][0]) for b in range(blocks)]
        transposed = far_products(
            False, row_side, far_row_src, far_col_dst, left, right, out_blocks=n_row * blocks
        )
        own = [forward[b * n_col : b * n_col + half] for b in range(blocks)]
        for step in range(1, len(col_masks) - 1):
            size = (own[0].shape[0] // 2, count_rhs, width)
            folded = call(
                fold_kernel, [(size, F32)] * (2 * blocks), "fold", [*own, *got], [transposed]
            )
            own = folded[:blocks]
            got = [swap(folded[blocks + b], "col", paths[b][step]) for b in range(blocks)]
            if step == 1:
                (transposed,) = near_products(
                    False, row_side, held, count, row_src, col_dst, start=transposed,
                    after=[folded[blocks]],
                )
        size = (own[0].shape[0] // 2 * blocks, count_rhs, width)
        col_size = (n_row * blocks // 2, count_rhs, width)
        own, send, col_own, col_send = call(
            join_kernel, [(size, F32)] * 2 + [(col_size, F32)] * 2, "join", [transposed, *own, *got]
        )
        row_terms = (own, swap(send, "col", col_masks[-1]))
        for step, mask in enumerate(scatter_row):
            if step:
                transposed = col_own + col_got
                half = transposed.shape[0] // 2
                col_own, col_send = transposed[:half], transposed[half:]
            col_got = swap(col_send, "row", mask)
        col_terms = (col_own, col_got)
        return [*row_terms, *col_terms], held

    devices = n_row * n_col
    full, packs = (count_rhs, columns), (blocks, count_rhs, width)
    shape_of = lambda wanted: pieces_shape(count_rhs, wanted, devices)
    partial = project(shape_of(rank), rhs, nys_factor)
    count = count.reshape(1)
    rhs, nys_factor, weight, self_row = stage([rhs, nys_factor, weight, self_row])
    proj = spread_sum(partial)
    direc, packed = call(
        begin_kernel, [(full, F32), (packs, BF16)], "begin", [rhs, weight, nys_factor, proj]
    )
    terms, tiles = operate(packed, near_tiles, True)
    image, partial = call(
        inner_kernel, [(full, F32), (shape_of(rank + 4 * count_rhs), F32)], "inner",
        [self_row, rhs, nys_factor, direc, *terms],
    )
    sums = spread_sum(partial)
    solution, residual, direc, packed, rho = call(
        advance_kernel,
        [(full, F32), (full, F32), (full, F32), (packs, BF16), ((count_rhs, count_rhs), F32)],
        "advance", [weight, nys_factor, rhs, sums, proj, direc, image],
    )
    terms, _ = operate(packed, tiles, False)
    image, partial = call(
        last_image_kernel, [(full, F32), ((count_rhs // 2, 2 * count_rhs), F32)], "last_image",
        [self_row, direc, *terms],
    )
    for mask in row_masks:
        partial = partial + swap(partial, "row", mask)
    gram = lax.all_to_all(
        jnp.broadcast_to(partial, (n_col, *partial.shape)), "col", 0, 0, tiled=True
    )
    return tuple(
        call(
            finish_kernel, [(full, F32), (full, F32)], "finish",
            [gram, rho, solution, residual, direc, image],
        )
    )


def solution(mesh):
    in_specs = (
        P(None, ("row", "col")),
        P(("row", "col")),
        P(("row", "col"), None, None),
        P(("row", "col")),
        P(("row", "col")),
        P(),
        P(("row", "col"), None, None),
        P(("row", "col"), None, None),
        P(("row", "col")),
        P(("row", "col")),
        P(None, ("row", "col")),
        P(),
    )
    out_specs = (P(None, ("row", "col")), P(None, ("row", "col")))
    return jax.shard_map(local, mesh=mesh, in_specs=in_specs, out_specs=out_specs, check_vma=False)
```

```python
import jax
import jax.numpy as jnp
from jax import lax
from jax.experimental import pallas as pl
from jax.experimental.pallas import tpu as pltpu
from jax.sharding import PartitionSpec as P

F32 = jnp.float32
BF16 = jnp.bfloat16
NN = (((1,), (0,)), ((), ()))
NT = (((1,), (1,)), ((), ()))
VMEM_LIMIT = 18 * 2**20
PROJECT_LIMIT = 62 * 2**20
STREAM_LIMIT = 36 * 2**20


def exact(left, right, dims):
    return lax.dot_general(
        left, right, dims, precision=lax.Precision.HIGHEST, preferred_element_type=F32
    )


def masks_of(axis):
    return [2**bit for bit in range(lax.axis_size(axis).bit_length() - 1)]


def swap(value, axis, mask):
    pairs = [(source, source ^ mask) for source in range(lax.axis_size(axis))]
    return lax.ppermute(value, axis, pairs)


def place(device, masks):
    spot = jnp.zeros_like(device)
    for mask in masks:
        spot = spot * 2 + (jnp.bitwise_and(device, mask) != 0).astype(jnp.int32)
    return spot


def pieces_shape(rows, columns, devices):
    return (devices, 2 * rows // devices, columns // 2)


def to_pieces(value, pieces_ref):
    pieces, depth, width = pieces_ref.shape
    for piece in range(pieces):
        row, half = piece // 2 * depth, piece % 2 * width
        pieces_ref[piece] = value[row : row + depth, half : half + width]


def from_pieces(pieces_ref):
    pieces = pieces_ref.shape[0]
    halves = [[pieces_ref[p] for p in range(side, pieces, 2)] for side in (0, 1)]
    return jnp.concatenate([jnp.concatenate(half, axis=0) for half in halves], axis=1)


def total_kernel(got_ref, out_ref):
    total = got_ref[0]
    for piece in range(1, got_ref.shape[0]):
        total = total + got_ref[piece]
    for piece in range(got_ref.shape[0]):
        out_ref[piece] = total


def spread_sum(pieces):
    axes = ("row", "col")
    got = lax.all_to_all(pieces, axes, 0, 0, tiled=True)
    (same,) = call(total_kernel, [(pieces.shape, F32)], "total", [got])
    return lax.all_to_all(same, axes, 0, 0, tiled=True)


def near_kernel(forward, chunk, stream, part, count_ref, src_ref, dst_ref, v_ref, tiles_ref, *refs):
    count = count_ref[0]
    chunks = lax.div(count + (chunk - 1), chunk)
    slots = tiles_ref.shape[0]
    if stream:
        out_ref, held_ref, arrived = refs

        def fetch(index):
            part = pl.ds(index * chunk, chunk)
            return pltpu.make_async_copy(
                tiles_ref.at[part], held_ref.at[part], arrived.at[index]
            )

        for index in range(slots // chunk):

            @pl.when(index < chunks)
            def _():
                fetch(index).start()

    else:
        out_ref, held_ref = refs[-1], tiles_ref
    out_ref[...] = jnp.zeros_like(out_ref) if stream or len(refs) == 1 else refs[0][...]

    first, last = (lax.min(chunks, slots // chunk * (part[0] + end) // part[1]) for end in (0, 1))

    def near(index, carry):
        if stream:
            fetch(index).wait()
        for s in range(chunk):
            tile = index * chunk + s
            v = v_ref[src_ref[tile]]
            v = jnp.where(tile < count, v, jnp.zeros_like(v))
            out_ref[dst_ref[tile]] += lax.dot_general(
                v, held_ref[tile], NT if forward else NN, preferred_element_type=F32
            )
        return carry

    lax.fori_loop(first, last, near, 0)
    if stream:

        def rest(index, carry):
            fetch(index).wait()
            return carry

        lax.fori_loop(last, chunks, rest, 0)


def near_products(
    forward, v, tiles, count, src, dst, part=(0, 1), out_blocks=None, start=None, stream=False, after=()
):
    slots, width, _ = tiles.shape
    rhs = v.shape[1]
    chunk = 32

    def body(*refs):
        near_kernel(forward, chunk, stream, part, *refs[len(after) :])

    extra = [] if start is None else [start]
    total = jax.ShapeDtypeStruct((out_blocks, rhs, width) if start is None else start.shape, F32)
    smem = pl.BlockSpec(memory_space=pltpu.SMEM)
    vmem = pl.BlockSpec(memory_space=pltpu.VMEM)
    hbm = pl.BlockSpec(memory_space=pltpu.HBM)
    return pl.pallas_call(
        body,
        out_shape=[total, jax.ShapeDtypeStruct(tiles.shape, tiles.dtype)] if stream else [total],
        in_specs=[pl.BlockSpec(memory_space=pl.ANY)] * len(after)
        + [smem] * 3
        + [vmem]
        + [hbm if stream else vmem]
        + [vmem] * len(extra),
        out_specs=[vmem, vmem] if stream else [vmem],
        scratch_shapes=[pltpu.SemaphoreType.DMA((slots // chunk,))] if stream else [],
        compiler_params=pltpu.CompilerParams(vmem_limit_bytes=STREAM_LIMIT if stream else VMEM_LIMIT),
        cost_estimate=pl.CostEstimate(
            flops=4 * slots * rhs * width * width,
            bytes_accessed=2 * slots * width * width,
            transcendentals=0,
        ),
        name="near_forward" if forward else "near_transposed",
    )(*after, count, src, dst, v, tiles, *extra)


def far_kernel(group, src_ref, dst_ref, v_ref, inner_ref, outer_ref, *refs):
    rhs = v_ref.shape[1]
    out_ref = refs[-1]
    if len(refs) == 2:
        out_ref[...] = refs[0][...]
    else:
        out_ref[...] = jnp.zeros_like(out_ref)
    panels = src_ref.shape[0]
    prank = inner_ref.shape[0] // panels
    shape = (group * rhs, group * prank)
    of_row = lax.div(lax.broadcasted_iota(jnp.int32, shape, 0), rhs)
    of_lane = lax.div(lax.broadcasted_iota(jnp.int32, shape, 1), prank)
    same = of_row == of_lane
    for start in range(0, panels, group):
        v = jnp.concatenate([v_ref[src_ref[start + g]] for g in range(group)], axis=0)
        part = pl.ds(start * prank, group * prank)
        half = lax.dot_general(v, inner_ref[part, :], NT, preferred_element_type=F32)
        half = jnp.where(same, half, 0.0).astype(BF16)
        prod = lax.dot_general(half, outer_ref[part, :], NN, preferred_element_type=F32)
        for g in range(group):
            out_ref[dst_ref[start + g]] += prod[g * rhs : (g + 1) * rhs]


def far_products(forward, v, src, dst, inner, outer, out_blocks=None, start=None, after=()):
    panels = src.shape[0]
    _, rhs, width = v.shape
    smem = pl.BlockSpec(memory_space=pltpu.SMEM)
    vmem = pl.BlockSpec(memory_space=pltpu.VMEM)
    extra = [] if start is None else [start]
    total = (out_blocks, rhs, width) if start is None else start.shape

    def body(*refs):
        far_kernel(8, *refs[len(after) :])

    return pl.pallas_call(
        body,
        out_shape=jax.ShapeDtypeStruct(total, F32),
        in_specs=[pl.BlockSpec(memory_space=pl.ANY)] * len(after)
        + [smem] * 2
        + [vmem] * (3 + len(extra)),
        out_specs=vmem,
        compiler_params=pltpu.CompilerParams(vmem_limit_bytes=VMEM_LIMIT),
        cost_estimate=pl.CostEstimate(
            flops=2 * panels * rhs * width * inner.shape[0] // panels,
            bytes_accessed=2 * inner.size,
            transcendentals=0,
        ),
        name="far_forward" if forward else "far_transposed",
    )(*after, src, dst, v, inner, outer, *extra)


def eliminate(systems, block=8):
    size, lanes = systems[0].shape
    parts = [[s[t : t + 8, :] for t in range(0, size, 8)] for s in systems]
    sub = lax.broadcasted_iota(jnp.int32, (8, lanes), 0)
    every = range(block)
    for k in range(0, size, block):
        home, offset = k // 8, k % 8
        for n, part in enumerate(parts):
            cols = [[jnp.broadcast_to(p[:, k + j : k + j + 1], p.shape) for p in part] for j in every]
            head = part[home]
            rows = [jnp.broadcast_to(head[offset + i : offset + i + 1, :], head.shape) for i in every]
            small = [
                [jnp.broadcast_to(cols[j][home][offset + i : offset + i + 1, :], head.shape) for j in every]
                for i in every
            ]
            for p in every:
                inverse = 1.0 / small[p][p]
                rows[p] = rows[p] * inverse
                for j in range(p + 1, block):
                    small[p][j] = small[p][j] * inverse
                for i in every:
                    if i != p:
                        factor = small[i][p]
                        rows[i] = rows[i] - factor * rows[p]
                        for j in range(p + 1, block):
                            small[i][j] = small[i][j] - factor * small[p][j]
            for t in range(len(part)):
                value = part[t]
                for j in every:
                    value = value - cols[j][t] * rows[j]
                part[t] = value
            for i in every:
                part[home] = jnp.where(sub == offset + i, rows[i], part[home])
    return [jnp.concatenate(part, axis=0)[:, size:] for part in parts]


def symmetric(matrix):
    return 0.5 * (matrix + matrix.T)


def call(kernel, outs, name, operands, after=(), limit=VMEM_LIMIT):
    vmem = pl.BlockSpec(memory_space=pltpu.VMEM)

    def body(*refs):
        kernel(*refs[len(after) :])

    return pl.pallas_call(
        body,
        out_shape=[jax.ShapeDtypeStruct(shape, dtype) for shape, dtype in outs],
        in_specs=[pl.BlockSpec(memory_space=pl.ANY)] * len(after) + [vmem] * len(operands),
        out_specs=[vmem] * len(outs),
        compiler_params=pltpu.CompilerParams(vmem_limit_bytes=limit),
        name=name,
    )(*after, *operands)


def pack(direc, packed_ref):
    blocks, _, width = packed_ref.shape
    for b in range(blocks):
        packed_ref[b] = direc[:, b * width : (b + 1) * width].astype(BF16)


def project_kernel(rhs_hbm, factor_hbm, out_ref, rhs, factor, arrived):
    parts = arrived.shape[0] - 1
    ranks = factor.shape[0] // parts
    copies = [pltpu.make_async_copy(rhs_hbm, rhs, arrived.at[parts])]
    for p in range(parts):
        part = pl.ds(p * ranks, ranks)
        copies.append(
            pltpu.make_async_copy(factor_hbm.at[part], factor.at[part], arrived.at[p])
        )
    for copy in copies:
        copy.start()
    copies[0].wait()
    resid = rhs[...]
    done = []
    for p in range(parts):
        copies[1 + p].wait()
        done.append(exact(factor[p * ranks : (p + 1) * ranks], resid, NT).T)
    to_pieces(jnp.concatenate(done, axis=1), out_ref)


def project(shape, rhs, factor):
    parts = 2
    return pl.pallas_call(
        project_kernel,
        out_shape=jax.ShapeDtypeStruct(shape, F32),
        in_specs=[pl.BlockSpec(memory_space=pltpu.HBM)] * 2,
        out_specs=pl.BlockSpec(memory_space=pltpu.VMEM),
        scratch_shapes=[
            pltpu.VMEM(rhs.shape, F32),
            pltpu.VMEM(factor.shape, F32),
            pltpu.SemaphoreType.DMA((parts + 1,)),
        ],
        compiler_params=pltpu.CompilerParams(vmem_limit_bytes=PROJECT_LIMIT),
        name="project",
    )(rhs, factor)


def stage_kernel(*refs):
    sources, held, arrived = refs[: len(refs) // 2], refs[len(refs) // 2 : -1], refs[-1]
    copies = [
        pltpu.make_async_copy(source, target, arrived.at[index])
        for index, (source, target) in enumerate(zip(sources, held))
    ]
    for copy in copies:
        copy.start()
    for copy in copies:
        copy.wait()


def stage(operands):
    return pl.pallas_call(
        stage_kernel,
        out_shape=[jax.ShapeDtypeStruct(value.shape, value.dtype) for value in operands],
        in_specs=[pl.BlockSpec(memory_space=pltpu.HBM)] * len(operands),
        out_specs=[pl.BlockSpec(memory_space=pltpu.VMEM)] * len(operands),
        scratch_shapes=[pltpu.SemaphoreType.DMA((len(operands),))],
        compiler_params=pltpu.CompilerParams(vmem_limit_bytes=VMEM_LIMIT),
        cost_estimate=pl.CostEstimate(flops=0, bytes_accessed=2**24, transcendentals=0),
        name="stage",
    )(*operands)


def begin_kernel(rhs, weight, factor, proj_ref, direc_ref, packed_ref):
    proj = from_pieces(proj_ref)
    direc = rhs[...] + exact(proj * weight[...], factor[...], NN)
    direc_ref[...] = direc
    pack(direc, packed_ref)


def image_of(self_term, direc, terms):
    both = terms[0][...] + terms[1][...] + terms[2][...] + terms[3][...]
    return self_term * direc + jnp.concatenate([both[b] for b in range(both.shape[0])], axis=1)


def copy_kernel(value_ref, out_ref):
    out_ref[...] = value_ref[...]


def fold_kernel(*refs):
    paths = len(refs) // 4
    own, got, keep, send = (refs[paths * index : paths * (index + 1)] for index in range(4))
    for p in range(paths):
        half = own[p].shape[0] // 2
        keep[p][...] = own[p][:half] + got[p][:half]
        send[p][...] = own[p][half:] + got[p][half:]


def join_kernel(transposed_ref, *refs):
    paths = len(refs) // 2 - 2
    keep, send, col_keep, col_send = refs[-4:]
    for p in range(paths):
        own, got = refs[p], refs[paths + p]
        half = own.shape[0] // 2
        part = pl.ds(p * half, half)
        keep[part] = own[:half] + got[:half]
        send[part] = own[half:] + got[half:]
    half = col_keep.shape[0]
    col_keep[...] = transposed_ref[:half]
    col_send[...] = transposed_ref[half:]


def inner_kernel(self_term, rhs, factor, direc_ref, *refs):
    terms, (image_ref, out_ref) = refs[:-2], refs[-2:]
    direc = direc_ref[...]
    image = image_of(self_term[...], direc, terms)
    image_ref[...] = image
    resid = rhs[...]
    count = resid.shape[0]
    stack = jnp.concatenate([direc, resid, image], axis=0)
    against = exact(stack, image, NT)
    own = exact(resid, resid, NT)
    pairs = jnp.concatenate(
        [against[:count], against[count : 2 * count], against[2 * count :], own], axis=1
    )
    to_pieces(jnp.concatenate([exact(image, factor[...], NT), pairs], axis=1), out_ref)


def advance_kernel(
    weight_ref,
    factor,
    rhs,
    sums_ref,
    proj_ref,
    direc_ref,
    image_ref,
    solution_ref,
    resid_ref,
    next_ref,
    packed_ref,
    rho_ref,
):
    count = rho_ref.shape[0]
    weight, proj, sums = weight_ref[...], from_pieces(proj_ref), from_pieces(sums_ref)
    rank = proj.shape[1]
    image_proj = sums[:, :rank]
    gram, cross, square, own = (
        sums[:, rank + count * index : rank + count * (index + 1)] for index in range(4)
    )
    rho = own + exact(proj * weight, proj, NT)
    unit = (
        lax.broadcasted_iota(jnp.int32, (count, count), 0)
        == lax.broadcasted_iota(jnp.int32, (count, count), 1)
    ).astype(F32)
    alpha, inverse = eliminate(
        [
            jnp.concatenate([symmetric(gram), rho], axis=1),
            jnp.concatenate([symmetric(rho), unit], axis=1),
        ]
    )
    alpha_t = alpha.T
    proj = proj - exact(alpha_t, image_proj, NN)
    mixed = exact(cross, alpha, NN)
    new = own - mixed - mixed.T + exact(exact(alpha_t, square, NN), alpha, NN)
    new = new + exact(proj * weight, proj, NT)
    beta = exact(inverse, new, NN)
    direc = direc_ref[...]
    resid = rhs[...] - exact(alpha_t, image_ref[...], NN)
    after = resid + exact(proj * weight, factor[...], NN) + exact(beta.T, direc, NN)
    pack(after, packed_ref)
    solution_ref[...] = exact(alpha_t, direc, NN)
    resid_ref[...] = resid
    next_ref[...] = after
    rho_ref[...] = new


def last_image_kernel(self_term, direc_ref, *refs):
    terms, (image_ref, gram_ref) = refs[:-2], refs[-2:]
    direc = direc_ref[...]
    image = image_of(self_term[...], direc, terms)
    image_ref[...] = image
    gram = exact(direc, image, NT)
    half = gram.shape[0] // 2
    gram_ref[...] = jnp.concatenate([gram[:half], gram[half:]], axis=1)


def finish_kernel(
    gram_ref, rho_ref, solution_ref, resid_ref, direc_ref, image_ref, out_ref, left_ref
):
    count = rho_ref.shape[0]
    gram = gram_ref[0]
    for index in range(1, gram_ref.shape[0]):
        gram = gram + gram_ref[index]
    gram = jnp.concatenate([gram[:, :count], gram[:, count:]], axis=0)
    (alpha,) = eliminate([jnp.concatenate([symmetric(gram), rho_ref[...]], axis=1)])
    alpha_t = alpha.T
    out_ref[...] = solution_ref[...] + exact(alpha_t, direc_ref[...], NN)
    left_ref[...] = resid_ref[...] - exact(alpha_t, image_ref[...], NN)


def local(
    rhs,
    self_term,
    near_tiles,
    near_rows,
    near_cols,
    near_counts,
    far_left,
    far_right,
    far_rows,
    far_cols,
    nys_factor,
    nys_weight,
):
    width = near_tiles.shape[1]
    count_rhs, columns = rhs.shape
    blocks = columns // width
    n_row, n_col = lax.axis_size("row"), lax.axis_size("col")
    grid_row, grid_col = lax.axis_index("row"), lax.axis_index("col")
    count = near_counts[grid_row * n_col + grid_col]
    rank = nys_factor.shape[0]
    self_row = self_term.reshape(1, columns)
    weight = nys_weight.reshape(1, rank)
    prank = far_left.shape[2]
    left = far_left.transpose(0, 2, 1).reshape(-1, width)
    right = far_right.transpose(0, 2, 1).reshape(-1, width)

    col_masks, row_masks = masks_of("col"), masks_of("row")
    gather_col, gather_row = col_masks[::-1], row_masks[::-1]
    path_a = col_masks[-2::-1] + col_masks[-1:]
    path_b = col_masks
    scatter_row = row_masks

    def relative(ids, me):
        return jnp.bitwise_xor(ids // blocks, me), ids % blocks

    def gathered(ids, me, masks):
        device, block = relative(ids, me)
        return place(device, masks[::-1]) * blocks + block

    def scattered_col(ids):
        device, block = relative(ids, grid_col)
        path = jnp.where(block % 2 == 0, place(device, path_a), place(device, path_b))
        return block * n_col + path

    def scattered_row(ids):
        device, block = relative(ids, grid_row)
        return place(device, scatter_row) * blocks + block

    row_src = gathered(near_rows, grid_col, gather_col)
    col_src = gathered(near_cols, grid_row, gather_row)
    far_row_src = gathered(far_rows, grid_col, gather_col)
    far_col_src = gathered(far_cols, grid_row, gather_row)
    row_dst, far_row_dst = scattered_col(near_rows), scattered_col(far_rows)
    col_dst, far_col_dst = scattered_row(near_cols), scattered_row(far_cols)

    def operate(packed, tiles, first):
        col_side = row_side = packed
        for mask in gather_row:
            col_side = jnp.concatenate([col_side, swap(col_side, "row", mask)], axis=0)
        (row_side,) = call(copy_kernel, [(packed.shape, BF16)], "gathered", [packed], [col_side])
        for mask in gather_col[:-2]:
            row_side = jnp.concatenate([row_side, swap(row_side, "col", mask)], axis=0)
        near = (count, col_src, row_dst)
        forward, *streamed = near_products(
            True, col_side, tiles, *near, part=(0, 2), out_blocks=n_col * blocks, stream=first
        )
        held = streamed[0] if first else tiles
        (row_side,) = call(
            copy_kernel, [(row_side.shape, BF16)], "gathered", [row_side], [forward]
        )
        other_side = swap(row_side, "col", gather_col[-2])
        (forward,) = near_products(
            True, col_side, held, *near, part=(1, 2), start=forward, after=[row_side]
        )
        row_side = jnp.concatenate([row_side, other_side], axis=0)
        (row_side,) = call(
            copy_kernel, [(row_side.shape, BF16)], "gathered", [row_side], [forward]
        )
        other_side = swap(row_side, "col", gather_col[-1])
        forward = far_products(
            True, col_side, far_col_src, far_row_dst, right, left, start=forward, after=[row_side]
        )
        row_side = jnp.concatenate([row_side, other_side], axis=0)

        half = n_col // 2
        sends = [forward[b * n_col + half : (b + 1) * n_col] for b in range(blocks)]
        paths = [path_a if b % 2 == 0 else path_b for b in range(blocks)]
        got = [swap(sends[b], "col", paths[b][0]) for b in range(blocks)]
        transposed = far_products(
            False, row_side, far_row_src, far_col_dst, left, right, out_blocks=n_row * blocks
        )
        own = [forward[b * n_col : b * n_col + half] for b in range(blocks)]
        for step in range(1, len(col_masks) - 1):
            size = (own[0].shape[0] // 2, count_rhs, width)
            folded = call(
                fold_kernel, [(size, F32)] * (2 * blocks), "fold", [*own, *got], [transposed]
            )
            own = folded[:blocks]
            got = [swap(folded[blocks + b], "col", paths[b][step]) for b in range(blocks)]
            if step == 1:
                (transposed,) = near_products(
                    False, row_side, held, count, row_src, col_dst, start=transposed,
                    after=[folded[blocks]],
                )
        size = (own[0].shape[0] // 2 * blocks, count_rhs, width)
        col_size = (n_row * blocks // 2, count_rhs, width)
        own, send, col_own, col_send = call(
            join_kernel, [(size, F32)] * 2 + [(col_size, F32)] * 2, "join", [transposed, *own, *got]
        )
        row_terms = (own, swap(send, "col", col_masks[-1]))
        for step, mask in enumerate(scatter_row):
            if step:
                transposed = col_own + col_got
                half = transposed.shape[0] // 2
                col_own, col_send = transposed[:half], transposed[half:]
            col_got = swap(col_send, "row", mask)
        col_terms = (col_own, col_got)
        return [*row_terms, *col_terms], held

    devices = n_row * n_col
    full, packs = (count_rhs, columns), (blocks, count_rhs, width)
    shape_of = lambda wanted: pieces_shape(count_rhs, wanted, devices)
    partial = project(shape_of(rank), rhs, nys_factor)
    count = count.reshape(1)
    rhs, nys_factor, weight, self_row = stage([rhs, nys_factor, weight, self_row])
    proj = spread_sum(partial)
    direc, packed = call(
        begin_kernel, [(full, F32), (packs, BF16)], "begin", [rhs, weight, nys_factor, proj]
    )
    terms, tiles = operate(packed, near_tiles, True)
    image, partial = call(
        inner_kernel, [(full, F32), (shape_of(rank + 4 * count_rhs), F32)], "inner",
        [self_row, rhs, nys_factor, direc, *terms],
    )
    sums = spread_sum(partial)
    solution, residual, direc, packed, rho = call(
        advance_kernel,
        [(full, F32), (full, F32), (full, F32), (packs, BF16), ((count_rhs, count_rhs), F32)],
        "advance", [weight, nys_factor, rhs, sums, proj, direc, image],
    )
    terms, _ = operate(packed, tiles, False)
    image, partial = call(
        last_image_kernel, [(full, F32), ((count_rhs // 2, 2 * count_rhs), F32)], "last_image",
        [self_row, direc, *terms],
    )
    for mask in row_masks:
        partial = partial + swap(partial, "row", mask)
    gram = lax.all_to_all(
        jnp.broadcast_to(partial, (n_col, *partial.shape)), "col", 0, 0, tiled=True
    )
    return tuple(
        call(
            finish_kernel, [(full, F32), (full, F32)], "finish",
            [gram, rho, solution, residual, direc, image],
        )
    )


def solution(mesh):
    in_specs = (
        P(None, ("row", "col")),
        P(("row", "col")),
        P(("row", "col"), None, None),
        P(("row", "col")),
        P(("row", "col")),
        P(),
        P(("row", "col"), None, None),
        P(("row", "col"), None, None),
        P(("row", "col")),
        P(("row", "col")),
        P(None, ("row", "col")),
        P(),
    )
    out_specs = (P(None, ("row", "col")), P(None, ("row", "col")))
    return jax.shard_map(local, mesh=mesh, in_specs=in_specs, out_specs=out_specs, check_vma=False)
```
